32 devices in a mesh: dp: 8 (over z, x), tensor: 4 (over y, core).
Axes of the slice: x: 2, y: 2, z: 4, core: 2. Of those that a mesh axis runs over, the one named last changes fastest.
Arguments:
- block_input: bfloat16 [64, 512, 768], P('dp', 'tensor'), may hold values from -6 to 6
- cotangent: bfloat16 [64, 512, 768], P('dp', 'tensor'), may hold values from -6 to 6
- segment_ids: int32 [64, 512], P('dp'), may hold values from 0 to 7, as said below
- rel_bucket: int32 [1023], replicated, may hold values from 0 to 31, as said below
- expert_route: int32 [64, 512], P('dp', 'tensor'), may hold values from 0 to 7
- expert_slot: int32 [64, 512], P('dp', 'tensor'), may hold values from -1 to 239, as said below
- attn_gain: bfloat16 [768], replicated, may hold values from 0.099609375 to 1.8984375
- moe_gain: bfloat16 [768], replicated, may hold values from 0.099609375 to 1.8984375
- router_weight: bfloat16 [768, 8], replicated, may hold values from -0.109375 to 0.109375
- rel_table: bfloat16 [32, 12], replicated, may hold values from -4 to 4
- w_query: bfloat16 [768, 768], P('dp', 'tensor'), may hold values from -0.02734375 to 0.02734375
- w_key: bfloat16 [768, 768], P('dp', 'tensor'), may hold values from -0.21875 to 0.21875
- w_value: bfloat16 [768, 768], P('dp', 'tensor'), may hold values from -0.21875 to 0.21875
- w_out: bfloat16 [768, 768], P('tensor', 'dp'), may hold values from -0.625 to 0.625
- expert_in: bfloat16 [8, 768, 3072], P('dp', None, 'tensor'), may hold values from -0.21875 to 0.21875
- expert_out: bfloat16 [8, 3072, 768], P('dp', 'tensor'), may hold values from -1.75 to 1.75
Outputs:
- block_output: bfloat16 [64, 512, 768], P('dp', 'tensor')
- input_grad: float32 [64, 512, 768], P('dp', 'tensor')
- attn_gain_grad: float32 [768], replicated
- moe_gain_grad: float32 [768], replicated
- router_grad: float32 [768, 8], replicated
- rel_table_grad: float32 [32, 12], replicated
- w_query_grad: float32 [768, 768], P('dp', 'tensor')
- w_key_grad: float32 [768, 768], P('dp', 'tensor')
- w_value_grad: float32 [768, 768], P('dp', 'tensor')
- w_out_grad: float32 [768, 768], P('tensor', 'dp')
- expert_in_grad: float32 [8, 768, 3072], P('dp', None, 'tensor')
- expert_out_grad: float32 [8, 3072, 768], P('dp', 'tensor')
The draws below stay inside these ranges and needn't reach their ends.
Inputs may be any that keep to these rules, and one draw needn't show every extreme that they name: `segment_ids`: segment numbers start at 0 in each sequence and never fall along it; in every group of 8 sequences of one index of dp one sequence is a single segment. `rel_bucket`: entry j - i + 511 holds the bucket of key j for query i; keys at or before the query use the lower half of the 32 buckets, keys after it the upper half, and buckets never fall as the distance grows. `expert_slot`: within the 1024 tokens of one device (its sequences in order, positions in order within each), a token's slot is the number of earlier tokens of that device routed to the same expert, or -1 once that number reaches 240; in every draw one expert receives 240 tokens from every device.
All inputs are finite; a program needn't handle non-finite values.
Results may differ from the reference program's by a relative error of at most 0.018.
Values may be sent and summed in bfloat16 or wider, within the bound.
No kernel may reach another device: no remote copies, remote signals or barrier semaphores. Data moves between devices by JAX's collectives and lax.ppermute only.
A program may use at most 256 MiB of HBM per device.

```python
import jax
import jax.numpy as jnp
from jax import lax

D = 768
H = 12
DH = 64
FF = 3072
NB = 32
LEN = 512
SEQ_GROUP = 8
EXPERTS = 8
SEQS = 64
TOK_DEV = 1024
CAP = 240
N_DP = 8
N_TENSOR = 4


def route_plan(key):
    subkeys = jax.random.split(key, 5)
    blocks_all = N_DP * N_TENSOR
    draw_first = jax.random.randint(subkeys[0], (blocks_all, TOK_DEV), 0, EXPERTS)
    second = jax.random.randint(subkeys[1], (blocks_all, TOK_DEV), 0, EXPERTS)
    relabel = jax.random.permutation(subkeys[2], EXPERTS)
    chosen = relabel[jnp.minimum(draw_first, second)]
    favored = jax.random.randint(subkeys[3], (), 0, EXPERTS)
    scores = jax.random.randint(subkeys[4], (blocks_all, TOK_DEV), 0, 4096) * TOK_DEV + jnp.arange(TOK_DEV)[None, :]
    rank_order = jnp.argsort(jnp.argsort(scores, axis=1, stable=True), axis=1, stable=True)
    chosen = jnp.where(rank_order < CAP, favored, chosen)
    onehot = (chosen[:, :, None] == jnp.arange(EXPERTS)[None, None, :]).astype(jnp.int32)
    running = jnp.cumsum(onehot, axis=1)
    position = jnp.sum(running * onehot, axis=2) - 1
    slot_table = jnp.where(position < CAP, position, -1)

    def arrange(grid_in):
        shaped = grid_in.reshape(N_DP, N_TENSOR, SEQ_GROUP, LEN // N_TENSOR)
        return shaped.transpose(0, 2, 1, 3).reshape(N_DP * SEQ_GROUP, LEN).astype(jnp.int32)
    return (arrange(chosen), arrange(slot_table))


def draw_expert_route(key, part):
    return route_plan(key)[0]


def draw_expert_slot(key, part):
    return route_plan(key)[1]


def draw_segment_ids(key, part):
    key = jax.random.fold_in(key, 11)
    subkeys = jax.random.split(key, 2)
    starts = jax.random.randint(subkeys[0], (N_DP * SEQ_GROUP, LEN), 0, LEN // 8) == 0
    marks = jnp.arange(LEN)
    forced = jnp.logical_and(marks % (LEN // 8) == 0, marks > 0)
    starts = jnp.logical_or(starts, forced[None, :])
    starts = starts.at[:, 0].set(False)
    single = jax.random.randint(subkeys[1], (N_DP, 1), 0, SEQ_GROUP)
    is_single = (jnp.arange(SEQ_GROUP)[None, :] == single).reshape(N_DP * SEQ_GROUP, 1)
    starts = jnp.logical_and(starts, jnp.logical_not(is_single))
    counted = jnp.cumsum(starts.astype(jnp.int32), axis=1)
    return jnp.minimum(counted, 7).astype(jnp.int32)


def draw_rel_bucket(key, part):
    key = jax.random.fold_in(key, 23)
    subkeys = jax.random.split(key, 2)
    half_count = NB // 2

    def levels(subkey):
        rises = (jax.random.randint(subkey, (LEN - 1,), 0, 4) == 0).astype(jnp.int32)
        climbed = jnp.minimum(jnp.cumsum(rises), half_count - 1)
        ending = jnp.where(jnp.arange(LEN - 1) == LEN - 2, half_count - 1, 0)
        return jnp.maximum(climbed, ending)
    after_side = half_count + levels(subkeys[0])
    before_side = levels(subkeys[1])
    return jnp.concatenate([before_side[::-1], jnp.zeros((1,), jnp.int32), after_side]).astype(jnp.int32)


def block_levels(rng, dims, pieces, low, largest):
    gain, own = 1.0, jax.random.fold_in(rng, 6)
    for dim, blocks in pieces:
        draws = jnp.exp(jax.random.uniform(jax.random.fold_in(own, dim), (blocks,), jnp.float32, low / len(pieces), largest / len(pieces)))
        gain = gain * jnp.repeat(draws, dims[dim] // blocks).reshape([-1 if axis == dim else 1 for axis in range(len(dims))])
    return gain


def scatter_about(stream_key, shape, scale, most, pieces=(), dtype=jnp.bfloat16):
    array = scale * jax.random.normal(stream_key, shape, jnp.float32)
    if pieces:
        array = array * block_levels(stream_key, shape, pieces, -0.22, 0.18)
    return jnp.clip(array, -most, most).astype(dtype)


def setup_inputs(seed: int = 0) -> dict:
    splits = jax.random.split(jax.random.key(seed), 17)
    block_input = scatter_about(splits[0], (SEQS, LEN, D), 1.0, 6.0, ((0, 8), (1, 4)))
    cotangent = scatter_about(splits[1], (SEQS, LEN, D), 1.0, 6.0, ((0, 8), (1, 4)))
    segment_ids = draw_segment_ids(jax.random.fold_in(splits[16], 71), 0)
    rel_bucket = draw_rel_bucket(jax.random.fold_in(splits[16], 71), 0)
    expert_route = draw_expert_route(jax.random.fold_in(splits[16], 71), 0)
    expert_slot = draw_expert_slot(jax.random.fold_in(splits[16], 71), 0)
    attn_gain = jnp.clip(1.0 + 0.18 * jax.random.normal(splits[6], (D,), jnp.float32), 0.099609375, 1.8984375).astype(jnp.bfloat16)
    moe_gain = jnp.clip(1.0 + 0.18 * jax.random.normal(splits[7], (D,), jnp.float32), 0.099609375, 1.8984375).astype(jnp.bfloat16)
    router_weight = scatter_about(splits[8], (D, EXPERTS), (4 * D) ** -0.5, 0.109375)
    rel_table = scatter_about(splits[9], (NB, H), 1.0, 4.0)
    w_query = scatter_about(splits[10], (D, H * DH), (D * DH) ** -0.5, 0.02734375, ((0, 8), (1, 4)))
    w_key = scatter_about(splits[11], (D, H * DH), D ** -0.5, 0.21875, ((0, 8), (1, 4)))
    w_value = scatter_about(splits[12], (D, H * DH), D ** -0.5, 0.21875, ((0, 8), (1, 4)))
    w_out = scatter_about(splits[13], (H * DH, D), (H * DH // 8) ** -0.5, 0.625, ((0, 4), (1, 8)))
    expert_in = scatter_about(splits[14], (EXPERTS, D, FF), D ** -0.5, 0.21875, ((0, 8), (2, 4)))
    expert_out = scatter_about(splits[15], (EXPERTS, FF, D), (max(1, FF // (4 * EXPERTS * EXPERTS))) ** -0.5, 1.75, ((0, 8), (1, 4)))
    return dict(block_input=block_input, cotangent=cotangent, segment_ids=segment_ids, rel_bucket=rel_bucket, expert_route=expert_route, expert_slot=expert_slot, attn_gain=attn_gain, moe_gain=moe_gain, router_weight=router_weight, rel_table=rel_table, w_query=w_query, w_key=w_key, w_value=w_value, w_out=w_out, expert_in=expert_in, expert_out=expert_out)


EPSILON = 1e-06
PRECISE = lax.Precision.HIGHEST

@jax.custom_vjp
def low(v):
    return lax.optimization_barrier(v.astype(jnp.bfloat16)).astype(jnp.float32)

@jax.custom_vjp
def low_back(v):
    return v

def low_keep(v):
    return (low(v), None)

def low_pass(kept, grad):
    return (grad,)

def back_keep(v):
    return (v, None)

def back_low(kept, grad):
    return (low(grad),)
low.defvjp(low_keep, low_pass)
low_back.defvjp(back_keep, back_low)

def attend_group(tokens_in, segments, attn_gain, rel_table, w_query, w_key, w_value, w_out, buckets):
    inverse_rms = lax.rsqrt(lax.optimization_barrier(jnp.mean(tokens_in * tokens_in, axis=-1, keepdims=True)) + EPSILON)
    normed = low(tokens_in * inverse_rms * attn_gain)

    def project(weight):
        projected = jnp.einsum('gld,de->gle', normed, weight, precision=PRECISE)
        return low(low_back(projected)).reshape(projected.shape[0], LEN, H, DH)
    queries = project(w_query)
    key_rows = project(w_key)
    value_rows = project(w_value)
    position_bias = jnp.transpose(rel_table[buckets], (2, 0, 1))
    logits = jnp.einsum('gihc,gjhc->ghij', queries, key_rows, precision=PRECISE) + position_bias[None]
    same_doc = segments[:, None, :, None] == segments[:, None, None, :]
    logits = low_back(jnp.where(same_doc, logits, -1e+30))
    peak_value = lax.optimization_barrier(jnp.max(logits, axis=-1, keepdims=True))
    expo = jnp.exp(logits - peak_value)
    attention_probabilities = low(expo / lax.optimization_barrier(jnp.sum(expo, axis=-1, keepdims=True)))
    attended = jnp.einsum('ghij,gjhc->gihc', attention_probabilities, value_rows, precision=PRECISE)
    attended = low(low_back(attended.reshape(attended.shape[0], LEN, H * DH)))
    branch_out = low_back(jnp.einsum('gle,ed->gld', attended, w_out, precision=PRECISE))
    return tokens_in + branch_out

def expert_apply(packed):
    inputs, w_first, w_second = packed
    pre_act = low_back(jnp.dot(inputs, w_first, precision=PRECISE, preferred_element_type=jnp.float32))
    hidden = low(jax.nn.gelu(pre_act))
    return low(low_back(jnp.dot(hidden, w_second, precision=PRECISE, preferred_element_type=jnp.float32)))

def reference(block_input, cotangent, segment_ids, rel_bucket, expert_route, expert_slot, attn_gain, moe_gain, router_weight, rel_table, w_query, w_key, w_value, w_out, expert_in, expert_out):
    across = jnp.arange(LEN)
    buckets = rel_bucket[across[None, :] - across[:, None] + LEN - 1]
    block_count = N_DP * N_TENSOR
    overflow = EXPERTS * block_count * CAP
    block_index = jnp.arange(SEQS)[:, None] // SEQ_GROUP * N_TENSOR + across[None, :] // (LEN // N_TENSOR)
    target = jnp.where(expert_slot >= 0, (expert_route * block_count + block_index) * CAP + expert_slot, overflow)
    target = target.reshape(-1).astype(jnp.int32)
    kept_mask = (expert_slot >= 0).astype(jnp.float32).reshape(-1, 1)
    fetch_index = jnp.minimum(target, overflow - 1).astype(jnp.int32)

    def forward(tokens_in, gain_one, gain_two, router, table, query_w, key_w, value_w, out_w, first_w, second_w):

        def attend(packed):
            return attend_group(packed[0], packed[1], gain_one, table, query_w, key_w, value_w, out_w, buckets)
        grouped = tokens_in.reshape(N_DP, SEQ_GROUP, LEN, D)
        grouped_segments = segment_ids.reshape(N_DP, SEQ_GROUP, LEN)
        after_attention = lax.map(jax.checkpoint(attend), (grouped, grouped_segments)).reshape(SEQS * LEN, D)
        inverse_rms = lax.rsqrt(lax.optimization_barrier(jnp.mean(after_attention * after_attention, axis=-1, keepdims=True)) + EPSILON)
        normed = after_attention * inverse_rms * gain_two
        logits = jnp.dot(normed, router, precision=PRECISE, preferred_element_type=jnp.float32)
        router_probs = jax.nn.softmax(logits, axis=-1)
        gate_value = jnp.take_along_axis(router_probs, expert_route.reshape(-1, 1), axis=-1)
        sent_rows = low(low_back(normed))
        buffer_rows = jnp.zeros((overflow, D), jnp.float32).at[target].set(sent_rows, mode='drop')
        outputs = lax.map(jax.checkpoint(expert_apply), (buffer_rows.reshape(EXPERTS, block_count * CAP, D), first_w, second_w))
        fetched = jnp.take(outputs.reshape(overflow, D), fetch_index, axis=0) * kept_mask
        return (after_attention + gate_value * fetched).reshape(SEQS, LEN, D)
    floats = (block_input.astype(jnp.float32), attn_gain.astype(jnp.float32), moe_gain.astype(jnp.float32), router_weight.astype(jnp.float32), rel_table.astype(jnp.float32), w_query.astype(jnp.float32), w_key.astype(jnp.float32), w_value.astype(jnp.float32), w_out.astype(jnp.float32), expert_in.astype(jnp.float32), expert_out.astype(jnp.float32))
    result, pullback = jax.vjp(forward, *floats)
    grads = pullback(cotangent.astype(jnp.float32))
    return (result.astype(jnp.bfloat16), grads[0], grads[1], grads[2], grads[3], grads[4], grads[5], grads[6], grads[7], grads[8], grads[9], grads[10])
```

```python
import functools

import jax
import jax.numpy as jnp
from jax import lax
from jax.experimental import pallas as pl
from jax.experimental.pallas import tpu as pltpu
from jax.sharding import PartitionSpec as P

EPSILON = 1e-06
MASKED_SCORE = -1e30
BF = jnp.bfloat16
F32 = jnp.float32
TILE = 128
NT = (((1,), (1,)), ((), ()))
TN = (((0,), (0,)), ((), ()))


def rms_inverse(values):
    return lax.rsqrt(jnp.mean(values * values, axis=-1, keepdims=True) + EPSILON)


def attn_norm(tokens_in, gain):
    return tokens_in * rms_inverse(tokens_in) * gain


def matmul(left, right, dims=None):
    if dims is None:
        dims = (((1,), (0,)), ((), ()))
    return lax.dot_general(left, right, dims, preferred_element_type=F32)


def head_only(rows, head, head_size):
    lane = lax.broadcasted_iota(jnp.int32, rows.shape, 1)
    inside = (lane >= head * head_size) & (lane < (head + 1) * head_size)
    return jnp.where(inside, rows, jnp.zeros_like(rows))


def attend_kernel(heads, head_size, n1_ref, w_ref, segc_ref, segr_ref, line_ref,
                  out_ref, qkv_ref, o_ref, p_ref, bias_ref, acc_ref):
    group, seq = pl.program_id(0), pl.program_id(1)
    width = heads * head_size
    model = n1_ref.shape[-1]
    length = segr_ref.shape[-1]
    tiles = length // TILE

    @pl.when(seq == 0)
    def _():
        for head in range(heads):
            for d in range(2 * tiles - 1):
                line = jnp.broadcast_to(line_ref[0, head, d : d + 1, :], (TILE, 2 * TILE))
                bias_ref[head, d] = pltpu.roll(line, 0, 1, stride=1, stride_axis=0)[:, TILE:]

    rows = n1_ref[:, 0].reshape(length, model)
    qkv = matmul(rows, w_ref[0, :, : 3 * width]).astype(BF)
    qkv_ref[0, 0] = qkv
    queries, keys, values = qkv[:, :width], qkv[:, width : 2 * width], qkv[:, 2 * width :]
    seg_row = segr_ref[0]
    attended = jnp.zeros((length, width), F32)
    for head in range(heads):
        scores = matmul(head_only(queries, head, head_size), keys, NT)
        for t in range(tiles):
            span = slice(t * TILE, (t + 1) * TILE)
            bias = jnp.concatenate(
                [bias_ref[head, c - t + tiles - 1] for c in range(tiles)], axis=1
            )
            same_doc = segc_ref[0, span] == seg_row
            part = jnp.where(same_doc, scores[span] + bias, MASKED_SCORE)
            peak = jnp.max(part, axis=1, keepdims=True)
            expo = jnp.exp(part - peak)
            total = jnp.sum(expo, axis=1, keepdims=True)
            p_ref[0, 0, head, span] = (expo * (1.0 / total)).astype(BF)
        attended += matmul(p_ref[0, 0, head], head_only(values, head, head_size))
    attended = attended.astype(BF)
    o_ref[0, 0] = attended
    branch = matmul(attended, w_ref[0, :, 3 * width :], NT)

    @pl.when(group == 0)
    def _():
        acc_ref[seq] = branch

    @pl.when(group > 0)
    def _():
        acc_ref[seq] += branch

    @pl.when(group == pl.num_programs(0) - 1)
    def _():
        out_ref[:, seq] = acc_ref[seq].astype(BF).reshape(tiles, TILE, model)


def attend_back_kernel(heads, head_size, n1_ref, db_ref, w_ref, qkv_ref, o_ref, p_ref,
                       out_ref, dw_ref, line_ref, gain_ref, acc_ref, dw_acc, sums_ref):
    group, seq = pl.program_id(0), pl.program_id(1)
    width = heads * head_size
    model = n1_ref.shape[-1]
    length = qkv_ref.shape[2]
    tiles = length // TILE
    rows = n1_ref[:, 0].reshape(length, model)
    branch_grad = db_ref[:, 0].reshape(length, model)
    attended_grad = matmul(branch_grad, w_ref[0, :, 3 * width :]).astype(BF)
    qkv = qkv_ref[0, 0]
    queries, keys, values = qkv[:, :width], qkv[:, width : 2 * width], qkv[:, 2 * width :]
    attended = o_ref[0, 0]
    queries_t = queries.T
    grad_t = attended_grad.T
    inner_all = attended_grad.astype(F32) * attended.astype(F32)

    @pl.when(seq == 0)
    def _():
        sums_ref[...] = jnp.zeros_like(sums_ref)

    query_grad = jnp.zeros((length, width), F32)
    key_grads, value_grads = [], []
    for head in range(heads):
        cut = slice(head * head_size, (head + 1) * head_size)
        inner = jnp.sum(head_only(inner_all, head, head_size), axis=1, keepdims=True)
        prob_grad = matmul(head_only(attended_grad, head, head_size), values, NT)
        probs = p_ref[0, 0, head]
        parts = []
        for t in range(tiles):
            span = slice(t * TILE, (t + 1) * TILE)
            part = probs[span].astype(F32) * (prob_grad[span] - inner[span])
            for c in range(tiles):
                sums_ref[head, c - t + tiles - 1] += part[:, c * TILE : (c + 1) * TILE]
            parts.append(part.astype(BF))
        score_grad = jnp.concatenate(parts, axis=0)
        query_grad += matmul(score_grad, head_only(keys, head, head_size))
        key_grads.append(matmul(queries_t[cut], score_grad))
        value_grads.append(matmul(grad_t[cut], probs))
    key_grad = jnp.concatenate(key_grads, axis=0).T
    value_grad = jnp.concatenate(value_grads, axis=0).T
    joined = jnp.concatenate(
        [query_grad.astype(BF), key_grad.astype(BF), value_grad.astype(BF)], axis=1
    )
    normed_grad = matmul(joined, w_ref[0, :, : 3 * width], NT)
    proj_grad = matmul(rows, joined, TN)
    out_grad = matmul(branch_grad, attended, TN)

    @pl.when(seq == 0)
    def _():
        dw_acc[:, : 3 * width] = proj_grad
        dw_acc[:, 3 * width :] = out_grad

    @pl.when(seq > 0)
    def _():
        dw_acc[:, : 3 * width] += proj_grad
        dw_acc[:, 3 * width :] += out_grad

    @pl.when(group == 0)
    def _():
        acc_ref[seq] = normed_grad

    @pl.when(group > 0)
    def _():
        acc_ref[seq] += normed_grad

    @pl.when(seq == pl.num_programs(1) - 1)
    def _():
        dw_ref[0] = dw_acc[...].astype(BF)
        row = lax.broadcasted_iota(jnp.int32, (TILE, TILE), 0)
        lane = lax.broadcasted_iota(jnp.int32, (TILE, TILE), 1)
        flip = (row + lane == TILE - 1).astype(F32)
        for head in range(heads):
            for d in range(2 * tiles - 1):
                turned = lax.dot_general(
                    flip, sums_ref[head, d], (((1,), (0,)), ((), ())),
                    precision=lax.Precision.HIGHEST, preferred_element_type=F32,
                )
                wide = jnp.concatenate([turned, jnp.zeros_like(turned)], axis=1)
                skewed = pltpu.roll(wide, 1, 1, stride=1, stride_axis=0)
                line_ref[0, head, d : d + 1, :] = jnp.sum(skewed, axis=0, keepdims=True)
            line_ref[0, head, 2 * tiles - 1 :, :] = jnp.zeros((1, 2 * TILE), F32)

    @pl.when((group == 0) & (seq == 0))
    def _():
        gain_ref[...] = jnp.zeros_like(gain_ref)

    @pl.when(group == pl.num_programs(0) - 1)
    def _():
        total = acc_ref[seq]
        out_ref[:, seq] = total.astype(BF).reshape(tiles, TILE, model)
        gain_ref[...] += jnp.sum(total * rows.astype(F32), axis=0, keepdims=True)


def expert_kernel(u_ref, c_ref, wi_ref, wo_ref, du_ref, dg_ref, r_ref, da_ref, acc_ref, dg_acc):
    chunk = pl.program_id(1)
    first, second = wi_ref[0], wo_ref[0]
    pre_act = matmul(u_ref[...], first)
    hidden_grad = matmul(c_ref[...], second, NT)
    root = 0.7978845608028654
    square = pre_act * pre_act
    bend = jnp.tanh(root * pre_act * (1.0 + 0.044715 * square))
    half = 0.5 * (1.0 + bend)
    hidden = (pre_act * half).astype(BF)
    slope = half + 0.5 * root * pre_act * (1.0 - bend * bend) * (1.0 + 3 * 0.044715 * square)
    pre_grad = (hidden_grad * slope).astype(BF)
    r_ref[0] = hidden
    da_ref[0] = pre_grad
    gate_part = jnp.sum(hidden.astype(F32) * hidden_grad, axis=1, keepdims=True)
    input_part = matmul(pre_grad, first, NT)

    @pl.when(chunk == 0)
    def _():
        acc_ref[...] = input_part
        dg_acc[...] = gate_part

    @pl.when(chunk > 0)
    def _():
        acc_ref[...] += input_part
        dg_acc[...] += gate_part

    @pl.when(chunk == pl.num_programs(1) - 1)
    def _():
        du_ref[...] = acc_ref[...].astype(BF)
        dg_ref[...] = dg_acc[...]


def attend(n1_seqs, weights, seg_here, lines, heads, head_size):
    groups, seqs, part, model = n1_seqs.shape
    length = seg_here.shape[1]
    width = heads * head_size
    tiles = length // TILE
    flops = 2 * groups * seqs * length * (4 * width * model + 2 * heads * length * head_size)
    return pl.pallas_call(
        functools.partial(attend_kernel, heads, head_size),
        grid=(groups, seqs),
        in_specs=[
            pl.BlockSpec((groups, 1, part, model), lambda g, s: (0, s, 0, 0)),
            pl.BlockSpec((1, model, 4 * width), lambda g, s: (g, 0, 0)),
            pl.BlockSpec((1, length, 1), lambda g, s: (s, 0, 0)),
            pl.BlockSpec((1, 1, length), lambda g, s: (s, 0, 0)),
            pl.BlockSpec((1, heads, 2 * tiles, 2 * TILE), lambda g, s: (g, 0, 0, 0)),
        ],
        out_specs=[
            pl.BlockSpec((groups, seqs, part, model), lambda g, s: (0, 0, 0, 0)),
            pl.BlockSpec((1, 1, length, 3 * width), lambda g, s: (g, s, 0, 0)),
            pl.BlockSpec((1, 1, length, width), lambda g, s: (g, s, 0, 0)),
            pl.BlockSpec((1, 1, heads, length, length), lambda g, s: (g, s, 0, 0, 0)),
        ],
        out_shape=[
            jax.ShapeDtypeStruct((groups, seqs, part, model), BF),
            jax.ShapeDtypeStruct((groups, seqs, length, 3 * width), BF),
            jax.ShapeDtypeStruct((groups, seqs, length, width), BF),
            jax.ShapeDtypeStruct((groups, seqs, heads, length, length), BF),
        ],
        scratch_shapes=[
            pltpu.VMEM((heads, 2 * tiles - 1, TILE, TILE), F32),
            pltpu.VMEM((seqs, length, model), F32),
        ],
        compiler_params=pltpu.CompilerParams(vmem_limit_bytes=48 << 20),
        cost_estimate=pl.CostEstimate(
            flops=6 * flops, bytes_accessed=24 << 20, transcendentals=groups * seqs * heads * length**2
        ),
        name="attend",
    )(n1_seqs, weights, seg_here[:, :, None], seg_here[:, None, :], lines)


def attend_back(n1_seqs, db_seqs, weights, qkv, attended, probs, heads, head_size):
    groups, seqs, part, model = n1_seqs.shape
    length = qkv.shape[2]
    width = heads * head_size
    tiles = length // TILE
    flops = 2 * groups * seqs * length * (8 * width * model + 4 * heads * length * head_size)
    return pl.pallas_call(
        functools.partial(attend_back_kernel, heads, head_size),
        grid=(groups, seqs),
        in_specs=[
            pl.BlockSpec((groups, 1, part, model), lambda g, s: (0, s, 0, 0)),
            pl.BlockSpec((groups, 1, part, model), lambda g, s: (0, s, 0, 0)),
            pl.BlockSpec((1, model, 4 * width), lambda g, s: (g, 0, 0)),
            pl.BlockSpec((1, 1, length, 3 * width), lambda g, s: (g, s, 0, 0)),
            pl.BlockSpec((1, 1, length, width), lambda g, s: (g, s, 0, 0)),
            pl.BlockSpec((1, 1, heads, length, length), lambda g, s: (g, s, 0, 0, 0)),
        ],
        out_specs=[
            pl.BlockSpec((groups, seqs, part, model), lambda g, s: (0, 0, 0, 0)),
            pl.BlockSpec((1, model, 4 * width), lambda g, s: (g, 0, 0)),
            pl.BlockSpec((1, heads, 2 * tiles, 2 * TILE), lambda g, s: (g, 0, 0, 0)),
            pl.BlockSpec((1, model), lambda g, s: (0, 0)),
        ],
        out_shape=[
            jax.ShapeDtypeStruct((groups, seqs, part, model), BF),
            jax.ShapeDtypeStruct((groups, model, 4 * width), BF),
            jax.ShapeDtypeStruct((groups, heads, 2 * tiles, 2 * TILE), F32),
            jax.ShapeDtypeStruct((1, model), F32),
        ],
        scratch_shapes=[
            pltpu.VMEM((seqs, length, model), F32),
            pltpu.VMEM((model, 4 * width), F32),
            pltpu.VMEM((heads, 2 * tiles - 1, TILE, TILE), F32),
        ],
        compiler_params=pltpu.CompilerParams(vmem_limit_bytes=56 << 20),
        cost_estimate=pl.CostEstimate(
            flops=6 * flops, bytes_accessed=32 << 20, transcendentals=0
        ),
        name="attend_back",
    )(n1_seqs, db_seqs, weights, qkv, attended, probs)


def run_experts(inputs, grads, first, second):
    rows, model = inputs.shape
    chunks, _, units = first.shape
    block = rows // 4
    flops = 2 * 3 * rows * model * units * chunks
    return pl.pallas_call(
        expert_kernel,
        grid=(rows // block, chunks),
        in_specs=[
            pl.BlockSpec((block, model), lambda b, k: (b, 0)),
            pl.BlockSpec((block, model), lambda b, k: (b, 0)),
            pl.BlockSpec((1, model, units), lambda b, k: (k, 0, 0)),
            pl.BlockSpec((1, units, model), lambda b, k: (k, 0, 0)),
        ],
        out_specs=[
            pl.BlockSpec((block, model), lambda b, k: (b, 0)),
            pl.BlockSpec((block, 1), lambda b, k: (b, 0)),
            pl.BlockSpec((1, block, units), lambda b, k: (k, b, 0)),
            pl.BlockSpec((1, block, units), lambda b, k: (k, b, 0)),
        ],
        out_shape=[
            jax.ShapeDtypeStruct((rows, model), BF),
            jax.ShapeDtypeStruct((rows, 1), F32),
            jax.ShapeDtypeStruct((chunks, rows, units), BF),
            jax.ShapeDtypeStruct((chunks, rows, units), BF),
        ],
        scratch_shapes=[pltpu.VMEM((block, model), F32), pltpu.VMEM((block, 1), F32)],
        compiler_params=pltpu.CompilerParams(vmem_limit_bytes=48 << 20),
        cost_estimate=pl.CostEstimate(
            flops=flops, bytes_accessed=60 << 20, transcendentals=rows * units * chunks
        ),
        name="experts",
    )(inputs, grads, first, second)


def swap_tensor(block, bit):
    size = lax.axis_size("tensor")
    return lax.ppermute(block, "tensor", [(i, i ^ bit) for i in range(size)])


def gather_tensor(block):
    pair = jnp.stack([block, swap_tensor(block, 2)])
    return jnp.concatenate([pair, swap_tensor(pair, 1)], axis=0)


def scatter_tensor(stack):
    near = swap_tensor(stack[2:], 1)
    kept = stack[0].astype(F32) + near[0].astype(F32)
    passed = (stack[1].astype(F32) + near[1].astype(F32)).astype(stack.dtype)
    return kept + swap_tensor(passed, 2).astype(F32)


def swap_dp(buffer):
    return lax.all_to_all(buffer, "dp", split_axis=0, concat_axis=0, tiled=True)


def swap_seqs(buffer):
    return lax.all_to_all(buffer, "tensor", split_axis=0, concat_axis=0, tiled=True)


def local(
    block_input,
    cotangent,
    segment_ids,
    rel_bucket,
    expert_route,
    expert_slot,
    attn_gain,
    moe_gain,
    router_weight,
    rel_table,
    w_query,
    w_key,
    w_value,
    w_out,
    expert_in,
    expert_out,
):
    group_seqs, part_len, model_width = block_input.shape
    tensor_size = lax.axis_size("tensor")
    dp_size = lax.axis_size("dp")
    full_len = part_len * tensor_size
    seqs_here = group_seqs // tensor_size
    head_cols = w_query.shape[1]
    weight_rows = w_query.shape[0]
    heads_all = rel_table.shape[1]
    heads_here = heads_all // tensor_size
    head_size = head_cols // heads_here
    bucket_count = rel_table.shape[0]
    experts_all = router_weight.shape[1]
    tok_rows = group_seqs * part_len
    capacity = tok_rows * 15 // (8 * experts_all)
    buffer_size = experts_all * capacity
    tiles = full_len // TILE
    me = lax.axis_index("tensor")
    visits = jnp.array([0, 2, 1, 3])
    order = me ^ visits

    packed = jnp.concatenate([w_query, w_key, w_value, w_out.T], axis=1)
    spread = jnp.broadcast_to(packed[None], (dp_size,) + packed.shape)
    owned = swap_dp(spread).reshape(model_width, 4 * head_cols)
    weights = gather_tensor(owned)

    flat_input = block_input.astype(F32)
    attn_gain_f = attn_gain.astype(F32)
    normed_local = attn_norm(flat_input, attn_gain_f).astype(BF)

    def by_seqs(rows):
        return swap_seqs(rows.reshape(tensor_size, seqs_here, part_len, model_width))

    n1_seqs = by_seqs(normed_local)
    seg_here = lax.dynamic_slice_in_dim(segment_ids, me * seqs_here, seqs_here, 0)
    bucket_onehot = (rel_bucket[:, None] == jnp.arange(bucket_count)[None, :]).astype(F32)
    bias_line = jnp.einsum(
        "kb,bh->hk", bucket_onehot, rel_table.astype(F32), precision=lax.Precision.HIGHEST
    )
    bias_line = jnp.pad(bias_line, ((0, 0), (1, 0))).reshape(heads_all, 2 * tiles, TILE)
    windows = jnp.concatenate([bias_line, jnp.roll(bias_line, -1, axis=1)], axis=2)
    windows = windows.reshape(tensor_size, heads_here, 2 * tiles, 2 * TILE)
    windows = jnp.take(windows, order, axis=0)

    route_rows = expert_route.reshape(tok_rows)
    slot_rows = expert_slot.reshape(tok_rows)
    slot_place = jnp.where(slot_rows >= 0, route_rows * capacity + slot_rows, buffer_size)
    slot_table = (slot_place[:, None] == jnp.arange(buffer_size)[None, :]).astype(BF)
    route_onehot = (route_rows[:, None] == jnp.arange(experts_all)[None, :]).astype(F32)

    def place_rows(rows):
        placed = jnp.einsum("tb,td->bd", slot_table, rows, preferred_element_type=F32)
        return placed.astype(BF).reshape(experts_all, capacity, model_width)

    def take_rows(buffer):
        return jnp.dot(
            slot_table, buffer.reshape(buffer_size, model_width), preferred_element_type=F32
        )

    cotangent_rows = cotangent.reshape(tok_rows, model_width)
    cotangent_arrived = swap_dp(place_rows(cotangent_rows)).reshape(buffer_size, model_width)
    first = gather_tensor(expert_in.reshape(model_width, -1))
    second = gather_tensor(expert_out.reshape(-1, model_width))

    branch, qkv, attended, probs = attend(
        n1_seqs, weights, seg_here, windows, heads_here, head_size
    )
    attn_branch = swap_seqs(branch).reshape(tok_rows, model_width).astype(F32)
    hidden_rows = flat_input.reshape(tok_rows, model_width) + attn_branch

    moe_gain_f = moe_gain.astype(F32)
    router_f = router_weight.astype(F32)
    rms = rms_inverse(hidden_rows)
    scaled = hidden_rows * rms
    normed_moe = scaled * moe_gain_f
    logits = jnp.dot(
        normed_moe, router_f, precision=lax.Precision.HIGHEST, preferred_element_type=F32
    )
    router_probs = jax.nn.softmax(logits, axis=-1)
    gate_value = jnp.sum(router_probs * route_onehot, axis=-1)

    arrived = swap_dp(place_rows(normed_moe.astype(BF))).reshape(buffer_size, model_width)
    slot_gate = jnp.sum(
        jnp.where(slot_place[:, None] == jnp.arange(buffer_size)[None, :], gate_value[:, None], 0.0),
        axis=0,
    )
    gate_arrived = swap_dp(slot_gate.reshape(experts_all, capacity)).reshape(buffer_size, 1)

    input_rows, gate_rows, hidden, pre_grad = run_experts(
        arrived, cotangent_arrived, first, second
    )
    input_back = swap_dp(input_rows.reshape(experts_all, capacity, model_width))
    gate_back = swap_dp(gate_rows.reshape(experts_all, capacity)).reshape(buffer_size)
    out_rows = jnp.einsum("krf,kfd->rd", hidden, second, preferred_element_type=F32).astype(BF)
    gated_c = (gate_arrived * cotangent_arrived.astype(F32)).astype(BF)
    gated_u = (gate_arrived * arrived.astype(F32)).astype(BF)
    second_terms = jnp.einsum("krf,rd->kfd", hidden, gated_c, preferred_element_type=F32).astype(BF)
    first_terms = jnp.einsum("rd,krf->kdf", gated_u, pre_grad, preferred_element_type=F32).astype(BF)
    second_grad = scatter_tensor(second_terms).reshape(expert_out.shape)
    first_grad = scatter_tensor(first_terms).reshape(expert_in.shape)

    out_grad = cotangent_rows.astype(F32)
    gate_grad = jnp.sum(
        jnp.where(slot_place[:, None] == jnp.arange(buffer_size)[None, :], gate_back[None, :], 0.0),
        axis=1,
    )
    logit_grad = (gate_grad * gate_value)[:, None] * (route_onehot - router_probs)
    router_part = lax.dot_general(
        normed_moe, logit_grad, TN, precision=lax.Precision.HIGHEST, preferred_element_type=F32
    )
    normed_grad = gate_value[:, None] * take_rows(input_back) + lax.dot_general(
        logit_grad, router_f, NT, precision=lax.Precision.HIGHEST, preferred_element_type=F32
    )
    moe_gain_part = jnp.sum(normed_grad * scaled, axis=0)
    gained = normed_grad * moe_gain_f
    residual_grad = (
        out_grad + rms * gained - scaled * rms * jnp.mean(gained * scaled, axis=-1, keepdims=True)
    )
    db_seqs = by_seqs(residual_grad.astype(BF))
    normed_back, weight_terms, line_sums, gain_sums = attend_back(
        n1_seqs, db_seqs, weights, qkv, attended, probs, heads_here, head_size
    )
    returned = swap_dp(out_rows.reshape(experts_all, capacity, model_width))
    block_output = (hidden_rows + gate_value[:, None] * take_rows(returned)).astype(BF)
    block_output = block_output.reshape(group_seqs, part_len, model_width)

    normed_back = swap_seqs(normed_back).reshape(group_seqs, part_len, model_width).astype(F32)
    gained_in = normed_back * attn_gain_f
    rms_in = rms_inverse(flat_input)
    scaled_in = flat_input * rms_in
    input_grad = (
        residual_grad.reshape(group_seqs, part_len, model_width)
        + rms_in * gained_in
        - scaled_in * rms_in * jnp.mean(gained_in * scaled_in, axis=-1, keepdims=True)
    )

    owner_terms = scatter_tensor(weight_terms).astype(BF)
    owner_terms = swap_dp(owner_terms.reshape(dp_size, weight_rows, 4 * head_cols))
    owner_grad = jnp.sum(owner_terms.astype(F32), axis=0)

    low, high = line_sums[..., :TILE], line_sums[..., TILE:]
    offset_sums = low + jnp.roll(high, 1, axis=2)
    offset_sums = offset_sums.reshape(heads_all, 2 * full_len)[:, 1:]
    table_part = jnp.einsum(
        "hk,kb->bh", offset_sums, bucket_onehot, precision=lax.Precision.HIGHEST
    ).reshape(bucket_count, tensor_size, heads_here)
    table_part = jnp.take(table_part, visits[me ^ jnp.arange(tensor_size)], axis=1).reshape(bucket_count, heads_all)
    attn_gain_grad, moe_gain_grad, router_grad, table_grad = lax.psum(
        (gain_sums[0] / attn_gain_f, moe_gain_part, router_part, table_part), ("dp", "tensor")
    )
    return (
        block_output,
        input_grad,
        attn_gain_grad,
        moe_gain_grad,
        router_grad,
        table_grad,
        owner_grad[:, :head_cols],
        owner_grad[:, head_cols : 2 * head_cols],
        owner_grad[:, 2 * head_cols : 3 * head_cols],
        owner_grad[:, 3 * head_cols :].T,
        first_grad,
        second_grad,
    )


def solution(mesh):
    in_specs = (
        P("dp", "tensor", None),
        P("dp", "tensor", None),
        P("dp", None),
        P(),
        P("dp", "tensor"),
        P("dp", "tensor"),
        P(),
        P(),
        P(),
        P(),
        P("dp", "tensor"),
        P("dp", "tensor"),
        P("dp", "tensor"),
        P("tensor", "dp"),
        P("dp", None, "tensor"),
        P("dp", "tensor", None),
    )
    out_specs = (
        P("dp", "tensor", None),
        P("dp", "tensor", None),
        P(),
        P(),
        P(),
        P(),
        P("dp", "tensor"),
        P("dp", "tensor"),
        P("dp", "tensor"),
        P("tensor", "dp"),
        P("dp", None, "tensor"),
        P("dp", "tensor", None),
    )
    return jax.shard_map(local, mesh=mesh, in_specs=in_specs, out_specs=out_specs, check_vma=False)
```

```python
import functools

import jax
import jax.numpy as jnp
from jax import lax
from jax.experimental import pallas as pl
from jax.experimental.pallas import tpu as pltpu
from jax.sharding import PartitionSpec as P

EPSILON = 1e-06
MASKED_SCORE = -1e30
BF = jnp.bfloat16
F32 = jnp.float32
TILE = 128
NT = (((1,), (1,)), ((), ()))
TN = (((0,), (0,)), ((), ()))


def rms_inverse(values):
    return lax.rsqrt(jnp.mean(values * values, axis=-1, keepdims=True) + EPSILON)


def attn_norm(tokens_in, gain):
    return tokens_in * rms_inverse(tokens_in) * gain


def matmul(left, right, dims=None):
    if dims is None:
        dims = (((1,), (0,)), ((), ()))
    return lax.dot_general(left, right, dims, preferred_element_type=F32)


def head_only(rows, head, head_size):
    lane = lax.broadcasted_iota(jnp.int32, rows.shape, 1)
    inside = (lane >= head * head_size) & (lane < (head + 1) * head_size)
    return jnp.where(inside, rows, jnp.zeros_like(rows))


def attend_kernel(heads, head_size, has_base, last, *refs):
    me_ref, n1_ref, segc_ref, segr_ref, line_ref = refs[:5]
    w_refs, refs = refs[5:7], refs[7:]
    if has_base:
        base_ref, refs = refs[0], refs[1:]
    if last:
        out_refs, refs = refs[:4], refs[4:]
        refs, total_all = refs[:-1], refs[-1]
    else:
        out_ref, refs = refs[0], refs[1:]
    qkv_ref, o_ref, p_ref, bias_ref = refs
    seq = pl.program_id(0)
    width = heads * head_size
    model = n1_ref.shape[-1]
    length = segr_ref.shape[-1]
    tiles = length // TILE

    @pl.when(seq == 0)
    def _():
        for group in range(2):
            for head in range(heads):
                for d in range(2 * tiles - 1):
                    line = jnp.broadcast_to(line_ref[group, head, d : d + 1, :], (TILE, 2 * TILE))
                    tile = pltpu.roll(line, 0, 1, stride=1, stride_axis=0)[:, TILE:]
                    bias_ref[group, head, d] = tile

    rows = n1_ref[:, 0].reshape(length, model)
    seg_row = segr_ref[0]
    branch = None
    for group in range(2):
        qkv = matmul(rows, w_refs[group][:, : 3 * width]).astype(BF)
        qkv_ref[group, 0] = qkv
        queries, keys, values = qkv[:, :width], qkv[:, width : 2 * width], qkv[:, 2 * width :]
        attended = jnp.zeros((length, width), F32)
        for head in range(heads):
            scores = matmul(head_only(queries, head, head_size), keys, NT)
            for t in range(tiles):
                span = slice(t * TILE, (t + 1) * TILE)
                bias = jnp.concatenate(
                    [bias_ref[group, head, c - t + tiles - 1] for c in range(tiles)], axis=1
                )
                same_doc = segc_ref[0, span] == seg_row
                part = jnp.where(same_doc, scores[span] + bias, MASKED_SCORE)
                peak = jnp.max(part, axis=1, keepdims=True)
                expo = jnp.exp(part - peak)
                total = jnp.sum(expo, axis=1, keepdims=True)
                p_ref[group, 0, head, span] = (expo * (1.0 / total)).astype(BF)
            attended += matmul(p_ref[group, 0, head], head_only(values, head, head_size))
        attended = attended.astype(BF)
        o_ref[group, 0] = attended
        term = matmul(attended, w_refs[group][:, 3 * width :], NT)
        branch = term if branch is None else branch + term
    if has_base:
        branch = branch + base_ref[0]
    if last:
        total_all[...] = branch
        part_len = n1_ref.shape[2]
        for k in range(4):
            start = pl.multiple_of((me_ref[0] ^ k) * part_len, part_len)
            out_refs[k][0] = total_all[pl.ds(start, part_len)].astype(BF)
    else:
        out_ref[0] = branch


def attend_back_kernel(heads, head_size, has_base, last, *refs):
    me_ref, n1_ref, qkv_ref, o_ref, p_ref = refs[:5]
    w_refs, db_refs, refs = refs[5:7], refs[7:11], refs[11:]
    if has_base:
        base_ref, refs = refs[0], refs[1:]
    if last:
        out_refs, refs = refs[:4], refs[4:]
    else:
        out_ref, refs = refs[0], refs[1:]
    dw_refs, line_ref, refs = refs[:2], refs[2], refs[3:]
    if last:
        gain_ref, refs = refs[0], refs[1:]
    dw_acc, sums_ref, db_all, total_all = refs
    seq = pl.program_id(0)
    part_len = n1_ref.shape[2]

    def place_of(k):
        return pl.ds(pl.multiple_of((me_ref[0] ^ k) * part_len, part_len), part_len)

    for k in range(4):
        db_all[place_of(k)] = db_refs[k][0]
    width = heads * head_size
    model = n1_ref.shape[-1]
    length = qkv_ref.shape[2]
    tiles = length // TILE
    rows = n1_ref[:, 0].reshape(length, model)
    branch_grad = db_all[...]

    @pl.when(seq == 0)
    def _():
        sums_ref[...] = jnp.zeros_like(sums_ref)
        dw_acc[...] = jnp.zeros_like(dw_acc)
        if last:
            gain_ref[...] = jnp.zeros_like(gain_ref)

    total = None
    for group in range(2):
        w_ref = w_refs[group]
        attended_grad = matmul(branch_grad, w_ref[:, 3 * width :]).astype(BF)
        qkv = qkv_ref[group, 0]
        queries, keys, values = qkv[:, :width], qkv[:, width : 2 * width], qkv[:, 2 * width :]
        attended = o_ref[group, 0]
        queries_t = queries.T
        grad_t = attended_grad.T
        inner_all = attended_grad.astype(F32) * attended.astype(F32)
        query_grad = jnp.zeros((length, width), F32)
        key_grads, value_grads = [], []
        for head in range(heads):
            cut = slice(head * head_size, (head + 1) * head_size)
            inner = jnp.sum(head_only(inner_all, head, head_size), axis=1, keepdims=True)
            prob_grad = matmul(head_only(attended_grad, head, head_size), values, NT)
            probs = p_ref[group, 0, head]
            parts = []
            for t in range(tiles):
                span = slice(t * TILE, (t + 1) * TILE)
                part = probs[span].astype(F32) * (prob_grad[span] - inner[span])
                for c in range(tiles):
                    tile = part[:, c * TILE : (c + 1) * TILE]
                    sums_ref[group, head, c - t + tiles - 1] += tile
                parts.append(part.astype(BF))
            score_grad = jnp.concatenate(parts, axis=0)
            query_grad += matmul(score_grad, head_only(keys, head, head_size))
            key_grads.append(matmul(queries_t[cut], score_grad))
            value_grads.append(matmul(grad_t[cut], probs))
        key_grad = jnp.concatenate(key_grads, axis=0).T
        value_grad = jnp.concatenate(value_grads, axis=0).T
        joined = jnp.concatenate(
            [query_grad.astype(BF), key_grad.astype(BF), value_grad.astype(BF)], axis=1
        )
        term = matmul(joined, w_ref[:, : 3 * width], NT)
        total = term if total is None else total + term
        dw_acc[group, :, : 3 * width] += matmul(rows, joined, TN)
        dw_acc[group, :, 3 * width :] += matmul(branch_grad, attended, TN)
    if has_base:
        total = total + base_ref[0]
    if last:
        total_all[...] = total
        for k in range(4):
            out_refs[k][0] = total_all[place_of(k)].astype(BF)
        gain_ref[...] += jnp.sum(total * rows.astype(F32), axis=0, keepdims=True)
    else:
        out_ref[0] = total

    @pl.when(seq == pl.num_programs(0) - 1)
    def _():
        row = lax.broadcasted_iota(jnp.int32, (TILE, TILE), 0)
        lane = lax.broadcasted_iota(jnp.int32, (TILE, TILE), 1)
        flip = (row + lane == TILE - 1).astype(F32)
        for group in range(2):
            dw_refs[group][...] = dw_acc[group].astype(BF)
            for head in range(heads):
                for d in range(2 * tiles - 1):
                    turned = lax.dot_general(
                        flip, sums_ref[group, head, d], (((1,), (0,)), ((), ())),
                        precision=lax.Precision.HIGHEST, preferred_element_type=F32,
                    )
                    wide = jnp.concatenate([turned, jnp.zeros_like(turned)], axis=1)
                    skewed = pltpu.roll(wide, 1, 1, stride=1, stride_axis=0)
                    line_ref[group, head, d : d + 1, :] = jnp.sum(skewed, axis=0, keepdims=True)
                line_ref[group, head, 2 * tiles - 1 :, :] = jnp.zeros((1, 2 * TILE), F32)


def expert_kernel(slots, u_ref, hg_ref, wi_ref, *refs):
    du_ref, r_ref, da_ref, acc_ref, dg_acc = refs[-5:]
    chunk = pl.program_id(1)
    first = wi_ref[0]
    sources, padded, model = u_ref.shape
    pre_act = matmul(u_ref[...].reshape(sources * padded, model), first)
    hidden_grad = hg_ref[0, :, 0].reshape(sources * padded, -1).astype(F32)
    root = 0.7978845608028654
    square = pre_act * pre_act
    bend = jnp.tanh(root * pre_act * (1.0 + 0.044715 * square))
    half = 0.5 * (1.0 + bend)
    hidden = (pre_act * half).astype(BF)
    slope = half + 0.5 * root * pre_act * (1.0 - bend * bend) * (1.0 + 3 * 0.044715 * square)
    pre_grad = (hidden_grad * slope).astype(BF)
    r_ref[0, :, 0] = hidden.reshape(sources, padded, -1)
    da_ref[0, :, 0] = pre_grad.reshape(sources, padded, -1)
    gate_part = jnp.sum(hidden.astype(F32) * hidden_grad, axis=1, keepdims=True)
    input_part = matmul(pre_grad, first, NT)

    @pl.when(chunk == 0)
    def _():
        acc_ref[...] = input_part
        dg_acc[...] = gate_part

    @pl.when(chunk > 0)
    def _():
        acc_ref[...] += input_part
        dg_acc[...] += gate_part

    @pl.when(chunk == pl.num_programs(1) - 1)
    def _():
        gates = jnp.broadcast_to(dg_acc[...], (sources * padded, TILE)).T[0:1]
        place = lax.broadcasted_iota(jnp.int32, (padded, model), 0)
        for source in range(sources):
            span = slice(source * padded, (source + 1) * padded)
            gate = gates[:, span]
            high = gate.astype(BF).astype(F32)
            extra = jnp.concatenate(
                [high, gate - high, jnp.zeros((1, model - 2 * padded), F32)], axis=1
            )
            du_ref[source] = jnp.where(place == slots, extra, acc_ref[span]).astype(BF)


def attend(me, n1_seqs, weights, seg_here, lines, base, heads, head_size):
    groups, seqs, part, model = n1_seqs.shape
    length = seg_here.shape[1]
    width = heads * head_size
    tiles = length // TILE
    last = base is not None
    flops = 2 * 2 * seqs * length * (4 * width * model + 2 * heads * length * head_size)
    whole = pl.BlockSpec((model, 4 * width), lambda s: (0, 0))
    rows_spec = pl.BlockSpec((1, length, model), lambda s: (s, 0, 0))
    seqs_spec = pl.BlockSpec((groups, 1, part, model), lambda s: (0, s, 0, 0))
    block_spec = pl.BlockSpec((1, part, model), lambda s: (s, 0, 0))
    return pl.pallas_call(
        functools.partial(attend_kernel, heads, head_size, last, last),
        grid=(seqs,),
        in_specs=[
            pl.BlockSpec(memory_space=pltpu.SMEM),
            seqs_spec,
            pl.BlockSpec((1, length, 1), lambda s: (s, 0, 0)),
            pl.BlockSpec((1, 1, length), lambda s: (s, 0, 0)),
            pl.BlockSpec((2, heads, 2 * tiles, 2 * TILE), lambda s: (0, 0, 0, 0)),
            whole,
            whole,
        ]
        + [rows_spec] * last,
        out_specs=[block_spec] * 4 * last
        + [rows_spec] * (not last)
        + [
            pl.BlockSpec((2, 1, length, 3 * width), lambda s: (0, s, 0, 0)),
            pl.BlockSpec((2, 1, length, width), lambda s: (0, s, 0, 0)),
            pl.BlockSpec((2, 1, heads, length, length), lambda s: (0, s, 0, 0, 0)),
        ],
        out_shape=[jax.ShapeDtypeStruct((seqs, part, model), BF)] * 4 * last
        + [jax.ShapeDtypeStruct((seqs, length, model), F32)] * (not last)
        + [
            jax.ShapeDtypeStruct((2, seqs, length, 3 * width), BF),
            jax.ShapeDtypeStruct((2, seqs, length, width), BF),
            jax.ShapeDtypeStruct((2, seqs, heads, length, length), BF),
        ],
        scratch_shapes=[pltpu.VMEM((2, heads, 2 * tiles - 1, TILE, TILE), F32)]
        + [pltpu.VMEM((length, model), F32)] * last,
        compiler_params=pltpu.CompilerParams(vmem_limit_bytes=48 << 20),
        cost_estimate=pl.CostEstimate(
            flops=3 * flops, bytes_accessed=12 << 20, transcendentals=2 * seqs * heads * length**2
        ),
        name="attend",
    )(me.reshape(1), n1_seqs, seg_here[:, :, None], seg_here[:, None, :], lines, *weights, *([base] * last))


def attend_back(me, n1_seqs, db_blocks, kept, weights, base, heads, head_size):
    qkv, attended, probs = kept
    groups, seqs, part, model = n1_seqs.shape
    length = qkv.shape[2]
    width = heads * head_size
    tiles = length // TILE
    last = base is not None
    flops = 2 * 2 * seqs * length * (8 * width * model + 4 * heads * length * head_size)
    whole = pl.BlockSpec((model, 4 * width), lambda s: (0, 0))
    rows_spec = pl.BlockSpec((1, length, model), lambda s: (s, 0, 0))
    seqs_spec = pl.BlockSpec((groups, 1, part, model), lambda s: (0, s, 0, 0))
    block_spec = pl.BlockSpec((1, part, model), lambda s: (s, 0, 0))
    dw_shape = jax.ShapeDtypeStruct((model, 4 * width), BF)
    return pl.pallas_call(
        functools.partial(attend_back_kernel, heads, head_size, last, last),
        grid=(seqs,),
        in_specs=[
            pl.BlockSpec(memory_space=pltpu.SMEM),
            seqs_spec,
            pl.BlockSpec((2, 1, length, 3 * width), lambda s: (0, s, 0, 0)),
            pl.BlockSpec((2, 1, length, width), lambda s: (0, s, 0, 0)),
            pl.BlockSpec((2, 1, heads, length, length), lambda s: (0, s, 0, 0, 0)),
            whole,
            whole,
        ]
        + [block_spec] * 4
        + [rows_spec] * last,
        out_specs=[block_spec] * 4 * last
        + [rows_spec] * (not last)
        + [
            whole,
            whole,
            pl.BlockSpec((2, heads, 2 * tiles, 2 * TILE), lambda s: (0, 0, 0, 0)),
        ]
        + [pl.BlockSpec((1, model), lambda s: (0, 0))] * last,
        out_shape=[jax.ShapeDtypeStruct((seqs, part, model), BF)] * 4 * last
        + [jax.ShapeDtypeStruct((seqs, length, model), F32)] * (not last)
        + [
            dw_shape,
            dw_shape,
            jax.ShapeDtypeStruct((2, heads, 2 * tiles, 2 * TILE), F32),
        ]
        + [jax.ShapeDtypeStruct((1, model), F32)] * last,
        scratch_shapes=[
            pltpu.VMEM((2, model, 4 * width), F32),
            pltpu.VMEM((2, heads, 2 * tiles - 1, TILE, TILE), F32),
            pltpu.VMEM((length, model), BF),
            pltpu.VMEM((length, model), F32),
        ],
        compiler_params=pltpu.CompilerParams(vmem_limit_bytes=56 << 20),
        cost_estimate=pl.CostEstimate(
            flops=2 * flops, bytes_accessed=16 << 20, transcendentals=0
        ),
        name="attend_back",
    )(me.reshape(1), n1_seqs, qkv, attended, probs, *weights, *db_blocks, *([base] * last))


def hidden_grads_kernel(c_ref, wo_ref, hg_ref):
    experts, halves, padded, model = c_ref.shape
    units = wo_ref.shape[1]
    grads = matmul(c_ref[...].reshape(experts * halves * padded, model), wo_ref[0], NT)
    hg_ref[0] = grads.astype(BF).reshape(experts, halves, padded, units)


def hidden_grads(grads, second):
    experts, halves, padded, model = grads.shape
    chunks, units, _ = second.shape
    sources = experts // 2
    return pl.pallas_call(
        hidden_grads_kernel,
        grid=(chunks, experts // sources),
        in_specs=[
            pl.BlockSpec((sources, halves, padded, model), lambda k, b: (b, 0, 0, 0)),
            pl.BlockSpec((1, units, model), lambda k, b: (k, 0, 0)),
        ],
        out_specs=pl.BlockSpec((1, sources, halves, padded, units), lambda k, b: (k, b, 0, 0, 0)),
        out_shape=jax.ShapeDtypeStruct((chunks, experts, halves, padded, units), BF),
        compiler_params=pltpu.CompilerParams(vmem_limit_bytes=48 << 20),
        cost_estimate=pl.CostEstimate(
            flops=2 * experts * halves * padded * model * units * chunks,
            bytes_accessed=20 << 20,
            transcendentals=0,
        ),
        name="hidden_grads",
    )(grads, second)


def expert_grads_kernel(gate_ref, ua_ref, ub_ref, c_ref, r_ref, da_ref, wo_ref,
                        y_ref, di_ref, di_near, do_ref, do_near,
                        y_acc, u_t, c_t, di_acc, do_acc):
    chunk, step = pl.program_id(0), pl.program_id(1)
    experts, halves, padded, model = c_ref.shape
    sources = experts // 2
    rows = sources * halves * padded
    units = wo_ref.shape[1]

    @pl.when(chunk == 0)
    def _():
        start = step * sources
        gate = gate_ref[pl.ds(pl.multiple_of(step * rows, rows), rows)]
        ua, ub = ua_ref[pl.ds(start, sources)], ub_ref[pl.ds(start, sources)]
        inputs = jnp.concatenate([ua[:, None], ub[:, None]], axis=1).reshape(rows, model)
        u_t[step] = (inputs.astype(F32) * gate).astype(BF).T
        grads = c_ref[pl.ds(start, sources)].reshape(rows, model)
        c_t[step] = (grads.astype(F32) * gate).astype(BF).T

    hidden = r_ref[0].reshape(rows, units)
    out_part = matmul(hidden, wo_ref[0])
    second_part = matmul(c_t[step], hidden)
    first_part = matmul(u_t[step], da_ref[0].reshape(rows, units))

    @pl.when(chunk == 0)
    def _():
        y_acc[step] = out_part

    @pl.when(chunk > 0)
    def _():
        y_acc[step] += out_part

    @pl.when(step == 0)
    def _():
        di_acc[...] = first_part
        do_acc[...] = second_part

    @pl.when((step == 1) & (chunk < 2))
    def _():
        di_ref[0] = (di_acc[...] + first_part).astype(BF)
        do_ref[0] = (do_acc[...] + second_part).T.astype(BF)

    @pl.when((step == 1) & (chunk >= 2))
    def _():
        di_near[0] = (di_acc[...] + first_part).astype(BF)
        do_near[0] = (do_acc[...] + second_part).T.astype(BF)

    @pl.when(chunk == pl.num_programs(0) - 1)
    def _():
        values = y_acc[step].astype(BF).reshape(sources, halves * padded, model)
        y_ref[pl.ds(step * sources, sources)] = values


def expert_grads(gates, u_first, u_second, grads, hidden, pre_grad, second):
    experts, halves, padded, model = grads.shape
    chunks, units, _ = second.shape
    sources = experts // 2
    rows = sources * halves * padded

    def whole(array):
        zeros = (0,) * array.ndim
        return pl.BlockSpec(array.shape, lambda k, b: zeros, pipeline_mode=pl.Buffered(1))

    kept_spec = pl.BlockSpec((1, sources, halves, padded, units), lambda k, b: (k, b, 0, 0, 0))
    own = pl.BlockSpec((1, model, units), lambda k, b: (jnp.minimum(k, 1), 0, 0))
    near = pl.BlockSpec((1, model, units), lambda k, b: (jnp.maximum(k - 2, 0), 0, 0))
    return pl.pallas_call(
        expert_grads_kernel,
        grid=(chunks, 2),
        in_specs=[
            whole(gates),
            whole(u_first),
            whole(u_second),
            whole(grads),
            kept_spec,
            kept_spec,
            pl.BlockSpec((1, units, model), lambda k, b: (k, 0, 0)),
        ],
        out_specs=[
            pl.BlockSpec((experts, halves * padded, model), lambda k, b: (0, 0, 0)),
            own,
            near,
            own,
            near,
        ],
        out_shape=[jax.ShapeDtypeStruct((experts, halves * padded, model), BF)]
        + [jax.ShapeDtypeStruct((2, model, units), BF)] * 4,
        scratch_shapes=[
            pltpu.VMEM((2, rows, model), F32),
            pltpu.VMEM((2, model, rows), BF),
            pltpu.VMEM((2, model, rows), BF),
            pltpu.VMEM((model, units), F32),
            pltpu.VMEM((model, units), F32),
        ],
        compiler_params=pltpu.CompilerParams(vmem_limit_bytes=60 << 20),
        cost_estimate=pl.CostEstimate(
            flops=4 * rows * model * units * chunks, bytes_accessed=40 << 20, transcendentals=0
        ),
        name="expert_grads",
    )(gates, u_first, u_second, grads, hidden, pre_grad, second)


def run_experts(half, slots, inputs, hidden_grad, first, kept):
    experts, padded, model = inputs.shape
    chunks, _, units = first.shape
    rows = experts * padded
    blocks = 2
    block = rows // blocks
    sources = experts // blocks
    kept_spec = pl.BlockSpec(
        (1, sources, 1, padded, units), lambda b, k: (k, b, half, 0, 0)
    )
    kept_shape = jax.ShapeDtypeStruct((chunks, experts, 2, padded, units), BF)
    return pl.pallas_call(
        functools.partial(expert_kernel, slots),
        grid=(blocks, chunks),
        in_specs=[
            pl.BlockSpec((sources, padded, model), lambda b, k: (b, 0, 0)),
            kept_spec,
            pl.BlockSpec((1, model, units), lambda b, k: (k, 0, 0)),
        ]
        + [pl.BlockSpec(memory_space=pl.ANY)] * len(kept),
        out_specs=[
            pl.BlockSpec((sources, padded, model), lambda b, k: (b, 0, 0)),
            kept_spec,
            kept_spec,
        ],
        out_shape=[jax.ShapeDtypeStruct((experts, padded, model), BF), kept_shape, kept_shape],
        scratch_shapes=[pltpu.VMEM((block, model), F32), pltpu.VMEM((block, 1), F32)],
        input_output_aliases={3 + i: 1 + i for i in range(len(kept))},
        compiler_params=pltpu.CompilerParams(vmem_limit_bytes=48 << 20),
        cost_estimate=pl.CostEstimate(
            flops=4 * rows * model * units * chunks, bytes_accessed=20 << 20, transcendentals=0
        ),
        name="experts",
    )(inputs, hidden_grad, first, *kept)


def swap_tensor(block, bit):
    size = lax.axis_size("tensor")
    return lax.ppermute(block, "tensor", [(i, i ^ bit) for i in range(size)])


def swap_dp(buffer):
    return lax.all_to_all(buffer, "dp", split_axis=0, concat_axis=0, tiled=True)


def swap_seqs(buffer):
    return lax.all_to_all(buffer, "tensor", split_axis=0, concat_axis=0, tiled=True)


def tie(*values):
    return lax.optimization_barrier(values)


def gather_dp(block):
    size, index = lax.axis_size("dp"), lax.axis_index("dp")
    found = block[None]
    bit = size // 2
    while bit:
        other = lax.ppermute(found, "dp", [(i, i ^ bit) for i in range(size)])
        upper = (index & bit) > 0
        pair = [jnp.where(upper, other, found), jnp.where(upper, found, other)]
        found = jnp.stack(pair, axis=1).reshape((-1,) + block.shape)
        bit //= 2
    return found


def scatter_dp(blocks):
    return jnp.sum(swap_dp(blocks).astype(F32), axis=0)


def sum_all(values):
    for axis in ("tensor", "dp"):
        size = lax.axis_size(axis)
        bit = 1
        while bit < size:
            values = values + lax.ppermute(values, axis, [(i, i ^ bit) for i in range(size)])
            bit *= 2
    return values


def by_xor(stack, index):
    pairs = jnp.concatenate([stack[1:2], stack[:1], stack[3:], stack[2:3]], axis=0)
    stack = jnp.where((index & 1) > 0, pairs, stack)
    return jnp.where((index & 2) > 0, jnp.concatenate([stack[2:], stack[:2]], axis=0), stack)


def local(
    block_input,
    cotangent,
    segment_ids,
    rel_bucket,
    expert_route,
    expert_slot,
    attn_gain,
    moe_gain,
    router_weight,
    rel_table,
    w_query,
    w_key,
    w_value,
    w_out,
    expert_in,
    expert_out,
):
    group_seqs, part_len, model_width = block_input.shape
    tensor_size = lax.axis_size("tensor")
    dp_size = lax.axis_size("dp")
    full_len = part_len * tensor_size
    seqs_here = group_seqs // tensor_size
    head_cols = w_query.shape[1]
    weight_rows = w_query.shape[0]
    heads_all = rel_table.shape[1]
    heads_here = heads_all // tensor_size
    head_size = head_cols // heads_here
    bucket_count = rel_table.shape[0]
    experts_all = router_weight.shape[1]
    tok_rows = group_seqs * part_len
    capacity = tok_rows * 15 // (8 * experts_all)
    half = capacity // 2
    padded = (half // 16 + 1) * 16
    half_size = experts_all * padded
    tiles = full_len // TILE
    me = lax.axis_index("tensor")

    packed = jnp.concatenate([w_query, w_key, w_value, w_out.T], axis=1)
    own_first = expert_in.reshape(model_width, -1)
    own_second = expert_out.reshape(-1, model_width)
    packed, tokens_in = tie(packed, block_input)
    w_own = gather_dp(packed).reshape(model_width, 4 * head_cols)
    w_core = swap_tensor(w_own, 1)
    w_far = swap_tensor(w_own, 2)

    flat_input = tokens_in.astype(F32)
    attn_gain_f = attn_gain.astype(F32)
    normed_local = attn_norm(flat_input, attn_gain_f).astype(BF)

    def by_seqs(rows):
        return swap_seqs(rows.reshape(tensor_size, seqs_here, part_len, model_width))

    n1_seqs = by_seqs(normed_local)
    seg_here = lax.dynamic_slice_in_dim(segment_ids, me * seqs_here, seqs_here, 0)
    bucket_onehot = (rel_bucket[:, None] == jnp.arange(bucket_count)[None, :]).astype(F32)
    bias_line = jnp.einsum(
        "kb,bh->hk", bucket_onehot, rel_table.astype(F32), precision=lax.Precision.HIGHEST
    )
    bias_line = jnp.pad(bias_line, ((0, 0), (1, 0))).reshape(heads_all, 2 * tiles, TILE)
    windows = jnp.concatenate([bias_line, jnp.roll(bias_line, -1, axis=1)], axis=2)
    windows = windows.reshape(tensor_size, heads_here, 2 * tiles, 2 * TILE)
    windows = by_xor(windows, me)

    route_rows = expert_route.reshape(tok_rows)
    slot_rows = expert_slot.reshape(tok_rows)
    upper = slot_rows >= half
    slot_place = jnp.where(
        slot_rows >= 0,
        route_rows * 2 * padded + slot_rows + upper * (padded - half),
        2 * half_size,
    )
    slot_ids = jnp.arange(2 * half_size).reshape(experts_all, 2, padded)

    def table_of(ids):
        return (slot_place[:, None] == ids.reshape(1, -1)).astype(BF)

    slot_tables = [table_of(slot_ids[:, h]) for h in range(2)]
    slot_table = table_of(slot_ids)
    route_onehot = (route_rows[:, None] == jnp.arange(experts_all)[None, :]).astype(F32)

    def place_rows(rows, h):
        placed = lax.dot_general(slot_tables[h], rows, TN, preferred_element_type=F32)
        return placed.reshape(experts_all, padded, model_width)

    def take_rows(buffers):
        return sum(
            matmul(slot_tables[h], buffers[h].reshape(half_size, -1)) for h in range(2)
        )

    def with_extra(placed, numbers, h):
        high = numbers.astype(BF)
        low = (numbers - high.astype(F32)).astype(BF)
        parts = lax.dot_general(jnp.stack([high, low]), slot_tables[h], (((1,), (0,)), ((), ())),
                                preferred_element_type=F32)
        parts = parts.reshape(2, experts_all, padded).transpose(1, 0, 2)
        parts = parts.reshape(experts_all, 1, 2 * padded)
        parts = jnp.pad(parts, ((0, 0), (0, 0), (0, model_width - 2 * padded)))
        at_extra = jnp.arange(padded)[None, :, None] == half
        return jnp.where(at_extra, parts, placed).astype(BF)

    def extra_of(buffer):
        row = buffer[:, half].astype(F32)
        return row[:, :padded] + row[:, padded : 2 * padded]

    cotangent_rows = cotangent.reshape(tok_rows, model_width)
    c_placed = lax.dot_general(slot_table, cotangent_rows, TN, preferred_element_type=F32)
    c_placed = c_placed.astype(BF).reshape(experts_all, 2 * padded, model_width)
    c_placed, n1_seqs, w_own = tie(c_placed, n1_seqs, w_own)
    c_arrived = swap_dp(c_placed)

    def stack_tensor(own, far):
        return jnp.stack([own, far, swap_tensor(own, 1), swap_tensor(far, 1)])

    partial, *kept_near = attend(
        me, n1_seqs, (w_own, w_core), seg_here, windows[:2], None, heads_here, head_size
    )
    partial, w_far, own_second = tie(partial, w_far, own_second)
    w_both = swap_tensor(w_far, 1)
    far_second = swap_tensor(own_second, 2)
    *branch, qkv_far, o_far, p_far = attend(
        me, n1_seqs, (w_far, w_both), seg_here, windows[2:], partial, heads_here, head_size
    )
    kept_far = (qkv_far, o_far, p_far)
    *branch, far_second = tie(*branch, far_second)
    branch = branch[:1] + [swap_tensor(branch[k], k) for k in range(1, 4)]
    *branch, c_arrived, own_first = tie(*branch, c_arrived, own_first)
    far_first = swap_tensor(own_first, 2)
    attn_branch = by_xor(jnp.stack(branch), me).reshape(tok_rows, model_width).astype(F32)
    hidden_rows = flat_input.reshape(tok_rows, model_width) + attn_branch
    second = stack_tensor(own_second, far_second)

    moe_gain_f = moe_gain.astype(F32)
    router_f = router_weight.astype(F32)
    rms = rms_inverse(hidden_rows)
    scaled = hidden_rows * rms
    normed_moe = scaled * moe_gain_f
    logits = jnp.dot(
        normed_moe, router_f, precision=lax.Precision.HIGHEST, preferred_element_type=F32
    )
    router_probs = jax.nn.softmax(logits, axis=-1)
    gate_value = jnp.sum(router_probs * route_onehot, axis=-1)

    sent_rows = normed_moe.astype(BF)
    u_placed = [with_extra(place_rows(sent_rows, h), gate_value, h) for h in range(2)]
    u_first = swap_dp(u_placed[0])
    c_all = c_arrived.reshape(experts_all, 2, padded, model_width)
    c_all, second, far_first = tie(c_all, second, far_first)
    first = stack_tensor(own_first, far_first)
    hidden_grad = hidden_grads(c_all, second)
    u_first, u_next, hidden_grad = tie(u_first, u_placed[1], hidden_grad)
    u_second = swap_dp(u_next)
    back_first, *kept = run_experts(0, half, u_first, hidden_grad, first, ())
    back_second, hidden, pre_grad = run_experts(1, half, u_second, hidden_grad, first, kept)
    back_first, u_second = tie(back_first, u_second)
    back_first = swap_dp(back_first)
    back_first, back_second = tie(back_first, back_second)
    back_second = swap_dp(back_second)

    gates = jnp.stack([extra_of(u_first), extra_of(u_second)], axis=1)[..., None]
    out_rows, first_terms, first_near, second_terms, second_near = expert_grads(
        gates.reshape(2 * half_size, 1), u_first, u_second, c_all, hidden, pre_grad, second
    )

    def near_sum(own, near):
        return own.astype(F32) + swap_tensor(near, 1).astype(F32)

    def near_terms(stack, near):
        near = swap_tensor(near, 1)
        passed = (stack[1].astype(F32) + near[1].astype(F32)).astype(BF)
        return passed, stack[0], near[0]

    first_passed, *first_parts = near_terms(first_terms, first_near)
    second_passed, *second_parts = near_terms(second_terms, second_near)

    out_grad = cotangent_rows.astype(F32)
    back_second, out_rows = tie(back_second, out_rows)
    returned = swap_dp(out_rows)
    gate_back = [extra_of(back_first), extra_of(back_second)]
    gate_back = [
        jnp.stack([v.astype(BF), (v - v.astype(BF).astype(F32)).astype(BF)], axis=-1)
        for v in gate_back
    ]
    gate_grad = jnp.sum(take_rows(gate_back), axis=-1)
    logit_grad = (gate_grad * gate_value)[:, None] * (route_onehot - router_probs)
    normed_grad = gate_value[:, None] * take_rows([back_first, back_second]) + lax.dot_general(
        logit_grad, router_f, NT, precision=lax.Precision.HIGHEST, preferred_element_type=F32
    )
    gained = normed_grad * moe_gain_f
    residual_grad = (
        out_grad + rms * gained - scaled * rms * jnp.mean(gained * scaled, axis=-1, keepdims=True)
    )
    db_rows = residual_grad.astype(BF).reshape(tensor_size, seqs_here, part_len, model_width)
    db_blocks = [lax.dynamic_index_in_dim(db_rows, me ^ k, 0, keepdims=False) for k in range(4)]
    db_blocks = db_blocks[:1] + [swap_tensor(db_blocks[k], k) for k in range(1, 4)]
    *db_blocks, first_passed = tie(*db_blocks, first_passed)
    first_far = swap_tensor(first_passed, 2)

    router_part = lax.dot_general(
        normed_moe, logit_grad, TN, precision=lax.Precision.HIGHEST, preferred_element_type=F32
    )
    moe_gain_part = jnp.sum(normed_grad * scaled, axis=0)

    partial, dw_far, dw_both, lines_far = attend_back(
        me, n1_seqs, db_blocks, kept_far, (w_far, w_both), None, heads_here, head_size
    )
    dw_both, first_far = tie(dw_both, first_far)
    far_term = near_sum(dw_far, dw_both).astype(BF)
    partial, far_term = tie(partial, far_term)
    far_term = swap_tensor(far_term, 2)
    *normed_back, dw_own, dw_core, lines_near, gain_sums = attend_back(
        me, n1_seqs, db_blocks, kept_near, (w_own, w_core), partial, heads_here, head_size
    )
    dw_core, far_term, returned = tie(dw_core, far_term, returned)
    owner_terms = (near_sum(dw_own, dw_core) + far_term.astype(F32)).astype(BF)
    owner_terms, gain_sums, lines_near = tie(owner_terms, gain_sums, lines_near)
    owner_grad = scatter_dp(owner_terms.reshape(dp_size, weight_rows, 4 * head_cols))

    normed_back = normed_back[:1] + [swap_tensor(normed_back[k], k) for k in range(1, 4)]
    *normed_back, second_passed, first_far = tie(*normed_back, second_passed, first_far)
    second_far = swap_tensor(second_passed, 2)
    first_grad = sum(v.astype(F32) for v in (*first_parts, first_far)).reshape(expert_in.shape)
    second_grad = sum(v.astype(F32) for v in (*second_parts, second_far))
    second_grad = second_grad.reshape(expert_out.shape)
    normed_back = by_xor(jnp.stack(normed_back), me)
    normed_back = normed_back.reshape(group_seqs, part_len, model_width).astype(F32)
    gained_in = normed_back * attn_gain_f
    rms_in = rms_inverse(flat_input)
    scaled_in = flat_input * rms_in
    input_grad = (
        residual_grad.reshape(group_seqs, part_len, model_width)
        + rms_in * gained_in
        - scaled_in * rms_in * jnp.mean(gained_in * scaled_in, axis=-1, keepdims=True)
    )
    block_output = hidden_rows + gate_value[:, None] * matmul(
        slot_table, returned.reshape(2 * half_size, model_width)
    )
    block_output = block_output.astype(BF).reshape(group_seqs, part_len, model_width)

    line_sums = by_xor(jnp.concatenate([lines_near, lines_far], axis=0), me)
    low, high = line_sums[..., :TILE], line_sums[..., TILE:]
    offset_sums = low + jnp.roll(high, 1, axis=2)
    offset_sums = offset_sums.reshape(heads_all, 2 * full_len)[:, 1:]
    table_part = jnp.einsum(
        "hk,kb->bh", offset_sums, bucket_onehot, precision=lax.Precision.HIGHEST
    )
    small = [gain_sums[0] / attn_gain_f, moe_gain_part, router_part, table_part]
    sums = jnp.concatenate([v.reshape(-1) for v in small])
    size = sums.size
    sums = jnp.pad(sums, (0, -size % (8 * TILE))).reshape(-1, TILE)
    sums = sum_all(sums).reshape(-1)
    totals, start = [], 0
    for v in small:
        totals.append(sums[start : start + v.size].reshape(v.shape))
        start += v.size
    return (
        block_output,
        input_grad,
        *totals,
        owner_grad[:, :head_cols],
        owner_grad[:, head_cols : 2 * head_cols],
        owner_grad[:, 2 * head_cols : 3 * head_cols],
        owner_grad[:, 3 * head_cols :].T,
        first_grad,
        second_grad,
    )


def solution(mesh):
    in_specs = (
        P("dp", "tensor", None),
        P("dp", "tensor", None),
        P("dp", None),
        P(),
        P("dp", "tensor"),
        P("dp", "tensor"),
        P(),
        P(),
        P(),
        P(),
        P("dp", "tensor"),
        P("dp", "tensor"),
        P("dp", "tensor"),
        P("tensor", "dp"),
        P("dp", None, "tensor"),
        P("dp", "tensor", None),
    )
    out_specs = (
        P("dp", "tensor", None),
        P("dp", "tensor", None),
        P(),
        P(),
        P(),
        P(),
        P("dp", "tensor"),
        P("dp", "tensor"),
        P("dp", "tensor"),
        P("tensor", "dp"),
        P("dp", None, "tensor"),
        P("dp", "tensor", None),
    )
    return jax.shard_map(local, mesh=mesh, in_specs=in_specs, out_specs=out_specs, check_vma=False)
```

```python
import functools

import jax
import jax.numpy as jnp
from jax import lax
from jax.experimental import pallas as pl
from jax.experimental.pallas import tpu as pltpu
from jax.sharding import PartitionSpec as P

EPSILON = 1e-06
MASKED_SCORE = -1e30
BF = jnp.bfloat16
F32 = jnp.float32
TILE = 128
NT = (((1,), (1,)), ((), ()))
TN = (((0,), (0,)), ((), ()))


def rms_inverse(values):
    return lax.rsqrt(jnp.mean(values * values, axis=-1, keepdims=True) + EPSILON)


def attn_norm(tokens_in, gain):
    return tokens_in * rms_inverse(tokens_in) * gain


def matmul(left, right, dims=None):
    if dims is None:
        dims = (((1,), (0,)), ((), ()))
    return lax.dot_general(left, right, dims, preferred_element_type=F32)


def head_only(rows, head, head_size):
    lane = lax.broadcasted_iota(jnp.int32, rows.shape, 1)
    inside = (lane >= head * head_size) & (lane < (head + 1) * head_size)
    return jnp.where(inside, rows, jnp.zeros_like(rows))


def attend_kernel(heads, head_size, has_base, last, *refs):
    me_ref, n1_ref, segc_ref, segr_ref, line_ref = refs[:5]
    w_refs, refs = refs[5:7], refs[7:]
    if has_base:
        base_ref, refs = refs[0], refs[1:]
    if last:
        out_refs, refs = refs[:4], refs[4:]
        refs, total_all = refs[:-1], refs[-1]
    else:
        out_ref, refs = refs[0], refs[1:]
    qkv_ref, o_ref, p_ref, bias_ref = refs
    seq = pl.program_id(0)
    width = heads * head_size
    model = n1_ref.shape[-1]
    length = segr_ref.shape[-1]
    tiles = length // TILE

    @pl.when(seq == 0)
    def _():
        for group in range(2):
            for head in range(heads):
                for d in range(2 * tiles - 1):
                    line = jnp.broadcast_to(line_ref[group, head, d : d + 1, :], (TILE, 2 * TILE))
                    tile = pltpu.roll(line, 0, 1, stride=1, stride_axis=0)[:, TILE:]
                    bias_ref[group, head, d] = tile

    rows = n1_ref[:, 0].reshape(length, model)
    seg_row = segr_ref[0]
    branch = None
    for group in range(2):
        qkv = matmul(rows, w_refs[group][:, : 3 * width]).astype(BF)
        qkv_ref[group, 0] = qkv
        queries, keys, values = qkv[:, :width], qkv[:, width : 2 * width], qkv[:, 2 * width :]
        attended = jnp.zeros((length, width), F32)
        for head in range(heads):
            scores = matmul(head_only(queries, head, head_size), keys, NT)
            for t in range(tiles):
                span = slice(t * TILE, (t + 1) * TILE)
                bias = jnp.concatenate(
                    [bias_ref[group, head, c - t + tiles - 1] for c in range(tiles)], axis=1
                )
                same_doc = segc_ref[0, span] == seg_row
                part = jnp.where(same_doc, scores[span] + bias, MASKED_SCORE)
                peak = jnp.max(part, axis=1, keepdims=True)
                expo = jnp.exp(part - peak)
                total = jnp.sum(expo, axis=1, keepdims=True)
                p_ref[group, 0, head, span] = (expo * (1.0 / total)).astype(BF)
            attended += matmul(p_ref[group, 0, head], head_only(values, head, head_size))
        attended = attended.astype(BF)
        o_ref[group, 0] = attended
        term = matmul(attended, w_refs[group][:, 3 * width :], NT)
        branch = term if branch is None else branch + term
    if has_base:
        branch = branch + base_ref[0]
    if last:
        total_all[...] = branch
        part_len = n1_ref.shape[2]
        for k in range(4):
            start = pl.multiple_of((me_ref[0] ^ k) * part_len, part_len)
            out_refs[k][0] = total_all[pl.ds(start, part_len)].astype(BF)
    else:
        out_ref[0] = branch


def attend_back_kernel(heads, head_size, has_base, last, *refs):
    me_ref, n1_ref, qkv_ref, o_ref, p_ref = refs[:5]
    w_refs, db_refs, refs = refs[5:7], refs[7:11], refs[11:]
    if has_base:
        base_ref, refs = refs[0], refs[1:]
    if last:
        out_refs, refs = refs[:4], refs[4:]
    else:
        out_ref, refs = refs[0], refs[1:]
    dw_refs, line_ref, refs = refs[:2], refs[2], refs[3:]
    if last:
        gain_ref, refs = refs[0], refs[1:]
    dw_acc, sums_ref, db_all, total_all = refs
    seq = pl.program_id(0)
    part_len = n1_ref.shape[2]

    def place_of(k):
        return pl.ds(pl.multiple_of((me_ref[0] ^ k) * part_len, part_len), part_len)

    for k in range(4):
        db_all[place_of(k)] = db_refs[k][0]
    width = heads * head_size
    model = n1_ref.shape[-1]
    length = qkv_ref.shape[2]
    tiles = length // TILE
    rows = n1_ref[:, 0].reshape(length, model)
    branch_grad = db_all[...]

    @pl.when(seq == 0)
    def _():
        sums_ref[...] = jnp.zeros_like(sums_ref)
        dw_acc[...] = jnp.zeros_like(dw_acc)
        if last:
            gain_ref[...] = jnp.zeros_like(gain_ref)

    total = None
    for group in range(2):
        w_ref = w_refs[group]
        attended_grad = matmul(branch_grad, w_ref[:, 3 * width :]).astype(BF)
        qkv = qkv_ref[group, 0]
        queries, keys, values = qkv[:, :width], qkv[:, width : 2 * width], qkv[:, 2 * width :]
        attended = o_ref[group, 0]
        queries_t = queries.T
        grad_t = attended_grad.T
        inner_all = attended_grad.astype(F32) * attended.astype(F32)
        query_grad = jnp.zeros((length, width), F32)
        key_grads, value_grads = [], []
        for head in range(heads):
            cut = slice(head * head_size, (head + 1) * head_size)
            inner = jnp.sum(head_only(inner_all, head, head_size), axis=1, keepdims=True)
            prob_grad = matmul(head_only(attended_grad, head, head_size), values, NT)
            probs = p_ref[group, 0, head]
            parts = []
            for t in range(tiles):
                span = slice(t * TILE, (t + 1) * TILE)
                part = probs[span].astype(F32) * (prob_grad[span] - inner[span])
                for c in range(tiles):
                    tile = part[:, c * TILE : (c + 1) * TILE]
                    sums_ref[group, head, c - t + tiles - 1] += tile
                parts.append(part.astype(BF))
            score_grad = jnp.concatenate(parts, axis=0)
            query_grad += matmul(score_grad, head_only(keys, head, head_size))
            key_grads.append(matmul(queries_t[cut], score_grad))
            value_grads.append(matmul(grad_t[cut], probs))
        key_grad = jnp.concatenate(key_grads, axis=0).T
        value_grad = jnp.concatenate(value_grads, axis=0).T
        joined = jnp.concatenate(
            [query_grad.astype(BF), key_grad.astype(BF), value_grad.astype(BF)], axis=1
        )
        term = matmul(joined, w_ref[:, : 3 * width], NT)
        total = term if total is None else total + term
        dw_acc[group, :, : 3 * width] += matmul(rows, joined, TN)
        dw_acc[group, :, 3 * width :] += matmul(branch_grad, attended, TN)
    if has_base:
        total = total + base_ref[0]
    if last:
        total_all[...] = total
        for k in range(4):
            out_refs[k][0] = total_all[place_of(k)].astype(BF)
        gain_ref[...] += jnp.sum(total * rows.astype(F32), axis=0, keepdims=True)
    else:
        out_ref[0] = total

    @pl.when(seq == pl.num_programs(0) - 1)
    def _():
        row = lax.broadcasted_iota(jnp.int32, (TILE, TILE), 0)
        lane = lax.broadcasted_iota(jnp.int32, (TILE, TILE), 1)
        flip = (row + lane == TILE - 1).astype(F32)
        for group in range(2):
            dw_refs[group][...] = dw_acc[group].astype(BF)
            for head in range(heads):
                for d in range(2 * tiles - 1):
                    turned = lax.dot_general(
                        flip, sums_ref[group, head, d], (((1,), (0,)), ((), ())),
                        precision=lax.Precision.HIGHEST, preferred_element_type=F32,
                    )
                    wide = jnp.concatenate([turned, jnp.zeros_like(turned)], axis=1)
                    skewed = pltpu.roll(wide, 1, 1, stride=1, stride_axis=0)
                    line_ref[group, head, d : d + 1, :] = jnp.sum(skewed, axis=0, keepdims=True)
                line_ref[group, head, 2 * tiles - 1 :, :] = jnp.zeros((1, 2 * TILE), F32)


def expert_kernel(slots, u_ref, hg_ref, wi_ref, *refs):
    du_ref, r_ref, da_ref, acc_ref, dg_acc = refs[-5:]
    chunk = pl.program_id(1)
    first = wi_ref[0]
    sources, padded, model = u_ref.shape
    pre_act = matmul(u_ref[...].reshape(sources * padded, model), first)
    hidden_grad = hg_ref[0, :, 0].reshape(sources * padded, -1).astype(F32)
    root = 0.7978845608028654
    square = pre_act * pre_act
    bend = jnp.tanh(root * pre_act * (1.0 + 0.044715 * square))
    half = 0.5 * (1.0 + bend)
    hidden = (pre_act * half).astype(BF)
    slope = half + 0.5 * root * pre_act * (1.0 - bend * bend) * (1.0 + 3 * 0.044715 * square)
    pre_grad = (hidden_grad * slope).astype(BF)
    r_ref[0, :, 0] = hidden.reshape(sources, padded, -1)
    da_ref[0, :, 0] = pre_grad.reshape(sources, padded, -1)
    gate_part = jnp.sum(hidden.astype(F32) * hidden_grad, axis=1, keepdims=True)
    input_part = matmul(pre_grad, first, NT)

    @pl.when(chunk == 0)
    def _():
        acc_ref[...] = input_part
        dg_acc[...] = gate_part

    @pl.when(chunk > 0)
    def _():
        acc_ref[...] += input_part
        dg_acc[...] += gate_part

    @pl.when(chunk == pl.num_programs(1) - 1)
    def _():
        gates = jnp.broadcast_to(dg_acc[...], (sources * padded, TILE)).T[0:1]
        place = lax.broadcasted_iota(jnp.int32, (padded, model), 0)
        for source in range(sources):
            span = slice(source * padded, (source + 1) * padded)
            gate = gates[:, span]
            high = gate.astype(BF).astype(F32)
            extra = jnp.concatenate(
                [high, gate - high, jnp.zeros((1, model - 2 * padded), F32)], axis=1
            )
            du_ref[source] = jnp.where(place == slots, extra, acc_ref[span]).astype(BF)


def attend(me, n1_seqs, weights, seg_here, lines, base, heads, head_size):
    groups, seqs, part, model = n1_seqs.shape
    length = seg_here.shape[1]
    width = heads * head_size
    tiles = length // TILE
    last = base is not None
    flops = 2 * 2 * seqs * length * (4 * width * model + 2 * heads * length * head_size)
    whole = pl.BlockSpec((model, 4 * width), lambda s: (0, 0))
    rows_spec = pl.BlockSpec((1, length, model), lambda s: (s, 0, 0))
    seqs_spec = pl.BlockSpec((groups, 1, part, model), lambda s: (0, s, 0, 0))
    block_spec = pl.BlockSpec((1, part, model), lambda s: (s, 0, 0))
    return pl.pallas_call(
        functools.partial(attend_kernel, heads, head_size, last, last),
        grid=(seqs,),
        in_specs=[
            pl.BlockSpec(memory_space=pltpu.SMEM),
            seqs_spec,
            pl.BlockSpec((1, length, 1), lambda s: (s, 0, 0)),
            pl.BlockSpec((1, 1, length), lambda s: (s, 0, 0)),
            pl.BlockSpec((2, heads, 2 * tiles, 2 * TILE), lambda s: (0, 0, 0, 0)),
            whole,
            whole,
        ]
        + [rows_spec] * last,
        out_specs=[block_spec] * 4 * last
        + [rows_spec] * (not last)
        + [
            pl.BlockSpec((2, 1, length, 3 * width), lambda s: (0, s, 0, 0)),
            pl.BlockSpec((2, 1, length, width), lambda s: (0, s, 0, 0)),
            pl.BlockSpec((2, 1, heads, length, length), lambda s: (0, s, 0, 0, 0)),
        ],
        out_shape=[jax.ShapeDtypeStruct((seqs, part, model), BF)] * 4 * last
        + [jax.ShapeDtypeStruct((seqs, length, model), F32)] * (not last)
        + [
            jax.ShapeDtypeStruct((2, seqs, length, 3 * width), BF),
            jax.ShapeDtypeStruct((2, seqs, length, width), BF),
            jax.ShapeDtypeStruct((2, seqs, heads, length, length), BF),
        ],
        scratch_shapes=[pltpu.VMEM((2, heads, 2 * tiles - 1, TILE, TILE), F32)]
        + [pltpu.VMEM((length, model), F32)] * last,
        compiler_params=pltpu.CompilerParams(vmem_limit_bytes=48 << 20),
        cost_estimate=pl.CostEstimate(
            flops=3 * flops, bytes_accessed=12 << 20, transcendentals=2 * seqs * heads * length**2
        ),
        name="attend",
    )(me.reshape(1), n1_seqs, seg_here[:, :, None], seg_here[:, None, :], lines, *weights, *([base] * last))


def attend_back(me, n1_seqs, db_blocks, kept, weights, base, heads, head_size):
    qkv, attended, probs = kept
    groups, seqs, part, model = n1_seqs.shape
    length = qkv.shape[2]
    width = heads * head_size
    tiles = length // TILE
    last = base is not None
    flops = 2 * 2 * seqs * length * (8 * width * model + 4 * heads * length * head_size)
    whole = pl.BlockSpec((model, 4 * width), lambda s: (0, 0))
    rows_spec = pl.BlockSpec((1, length, model), lambda s: (s, 0, 0))
    seqs_spec = pl.BlockSpec((groups, 1, part, model), lambda s: (0, s, 0, 0))
    block_spec = pl.BlockSpec((1, part, model), lambda s: (s, 0, 0))
    dw_shape = jax.ShapeDtypeStruct((model, 4 * width), BF)
    return pl.pallas_call(
        functools.partial(attend_back_kernel, heads, head_size, last, last),
        grid=(seqs,),
        in_specs=[
            pl.BlockSpec(memory_space=pltpu.SMEM),
            seqs_spec,
            pl.BlockSpec((2, 1, length, 3 * width), lambda s: (0, s, 0, 0)),
            pl.BlockSpec((2, 1, length, width), lambda s: (0, s, 0, 0)),
            pl.BlockSpec((2, 1, heads, length, length), lambda s: (0, s, 0, 0, 0)),
            whole,
            whole,
        ]
        + [block_spec] * 4
        + [rows_spec] * last,
        out_specs=[block_spec] * 4 * last
        + [rows_spec] * (not last)
        + [
            whole,
            whole,
            pl.BlockSpec((2, heads, 2 * tiles, 2 * TILE), lambda s: (0, 0, 0, 0)),
        ]
        + [pl.BlockSpec((1, model), lambda s: (0, 0))] * last,
        out_shape=[jax.ShapeDtypeStruct((seqs, part, model), BF)] * 4 * last
        + [jax.ShapeDtypeStruct((seqs, length, model), F32)] * (not last)
        + [
            dw_shape,
            dw_shape,
            jax.ShapeDtypeStruct((2, heads, 2 * tiles, 2 * TILE), F32),
        ]
        + [jax.ShapeDtypeStruct((1, model), F32)] * last,
        scratch_shapes=[
            pltpu.VMEM((2, model, 4 * width), F32),
            pltpu.VMEM((2, heads, 2 * tiles - 1, TILE, TILE), F32),
            pltpu.VMEM((length, model), BF),
            pltpu.VMEM((length, model), F32),
        ],
        compiler_params=pltpu.CompilerParams(vmem_limit_bytes=56 << 20),
        cost_estimate=pl.CostEstimate(
            flops=2 * flops, bytes_accessed=16 << 20, transcendentals=0
        ),
        name="attend_back",
    )(me.reshape(1), n1_seqs, qkv, attended, probs, *weights, *db_blocks, *([base] * last))


def hidden_grads_kernel(c_ref, wo_ref, hg_ref):
    experts, halves, padded, model = c_ref.shape
    units = wo_ref.shape[1]
    grads = matmul(c_ref[...].reshape(experts * halves * padded, model), wo_ref[0], NT)
    hg_ref[0] = grads.astype(BF).reshape(experts, halves, padded, units)


def hidden_grads(grads, second):
    experts, halves, padded, model = grads.shape
    chunks, units, _ = second.shape
    sources = experts // 2
    return pl.pallas_call(
        hidden_grads_kernel,
        grid=(chunks, experts // sources),
        in_specs=[
            pl.BlockSpec((sources, halves, padded, model), lambda k, b: (b, 0, 0, 0)),
            pl.BlockSpec((1, units, model), lambda k, b: (k, 0, 0)),
        ],
        out_specs=pl.BlockSpec((1, sources, halves, padded, units), lambda k, b: (k, b, 0, 0, 0)),
        out_shape=jax.ShapeDtypeStruct((chunks, experts, halves, padded, units), BF),
        compiler_params=pltpu.CompilerParams(vmem_limit_bytes=48 << 20),
        cost_estimate=pl.CostEstimate(flops=1, bytes_accessed=1, transcendentals=0),
        name="hidden_grads",
    )(grads, second)


def expert_grads_kernel(gate_ref, ua_ref, ub_ref, c_ref, r_ref, da_ref,
                        di_ref, di_near, do_ref, do_near, u_t, c_t, di_acc, do_acc):
    chunk, step = pl.program_id(0), pl.program_id(1)
    experts, halves, padded, model = c_ref.shape
    sources = experts // 2
    rows = sources * halves * padded
    units = r_ref.shape[-1]

    @pl.when(chunk == 0)
    def _():
        start = step * sources
        gate = gate_ref[pl.ds(pl.multiple_of(step * rows, rows), rows)]
        ua, ub = ua_ref[pl.ds(start, sources)], ub_ref[pl.ds(start, sources)]
        inputs = jnp.concatenate([ua[:, None], ub[:, None]], axis=1).reshape(rows, model)
        u_t[step] = (inputs.astype(F32) * gate).astype(BF).T
        grads = c_ref[pl.ds(start, sources)].reshape(rows, model)
        c_t[step] = (grads.astype(F32) * gate).astype(BF).T

    hidden = r_ref[0].reshape(rows, units)
    second_part = matmul(c_t[step], hidden)
    first_part = matmul(u_t[step], da_ref[0].reshape(rows, units))

    @pl.when(step == 0)
    def _():
        di_acc[...] = first_part
        do_acc[...] = second_part

    @pl.when((step == 1) & (chunk < 2))
    def _():
        di_ref[0] = (di_acc[...] + first_part).astype(BF)
        do_ref[0] = (do_acc[...] + second_part).T.astype(BF)

    @pl.when((step == 1) & (chunk >= 2))
    def _():
        di_near[0] = (di_acc[...] + first_part).astype(BF)
        do_near[0] = (do_acc[...] + second_part).T.astype(BF)


def expert_grads(gates, u_first, u_second, grads, hidden, pre_grad):
    experts, halves, padded, model = grads.shape
    chunks, units = hidden.shape[0], hidden.shape[-1]
    sources = experts // 2
    rows = sources * halves * padded

    def whole(array):
        zeros = (0,) * array.ndim
        return pl.BlockSpec(array.shape, lambda k, b: zeros, pipeline_mode=pl.Buffered(1))

    kept_spec = pl.BlockSpec((1, sources, halves, padded, units), lambda k, b: (k, b, 0, 0, 0))
    own = pl.BlockSpec((1, model, units), lambda k, b: (jnp.minimum(k, 1), 0, 0))
    near = pl.BlockSpec((1, model, units), lambda k, b: (jnp.maximum(k - 2, 0), 0, 0))
    return pl.pallas_call(
        expert_grads_kernel,
        grid=(chunks, 2),
        in_specs=[
            whole(gates),
            whole(u_first),
            whole(u_second),
            whole(grads),
            kept_spec,
            kept_spec,
        ],
        out_specs=[
            own,
            near,
            own,
            near,
        ],
        out_shape=[jax.ShapeDtypeStruct((2, model, units), BF)] * 4,
        scratch_shapes=[
            pltpu.VMEM((2, model, rows), BF),
            pltpu.VMEM((2, model, rows), BF),
            pltpu.VMEM((model, units), F32),
            pltpu.VMEM((model, units), F32),
        ],
        compiler_params=pltpu.CompilerParams(vmem_limit_bytes=60 << 20),
        cost_estimate=pl.CostEstimate(
            flops=8 * rows * model * units * chunks, bytes_accessed=40 << 20, transcendentals=0
        ),
        name="expert_grads",
    )(gates, u_first, u_second, grads, hidden, pre_grad)


def run_experts(half, slots, inputs, hidden_grad, first, kept):
    experts, padded, model = inputs.shape
    chunks, _, units = first.shape
    rows = experts * padded
    blocks = 2
    block = rows // blocks
    sources = experts // blocks
    kept_spec = pl.BlockSpec(
        (1, sources, 1, padded, units), lambda b, k: (k, b, half, 0, 0)
    )
    kept_shape = jax.ShapeDtypeStruct((chunks, experts, 2, padded, units), BF)
    return pl.pallas_call(
        functools.partial(expert_kernel, slots),
        grid=(blocks, chunks),
        in_specs=[
            pl.BlockSpec((sources, padded, model), lambda b, k: (b, 0, 0)),
            kept_spec,
            pl.BlockSpec((1, model, units), lambda b, k: (k, 0, 0)),
        ]
        + [pl.BlockSpec(memory_space=pl.ANY)] * len(kept),
        out_specs=[
            pl.BlockSpec((sources, padded, model), lambda b, k: (b, 0, 0)),
            kept_spec,
            kept_spec,
        ],
        out_shape=[jax.ShapeDtypeStruct((experts, padded, model), BF), kept_shape, kept_shape],
        scratch_shapes=[pltpu.VMEM((block, model), F32), pltpu.VMEM((block, 1), F32)],
        input_output_aliases={3 + i: 1 + i for i in range(len(kept))},
        compiler_params=pltpu.CompilerParams(vmem_limit_bytes=48 << 20),
        cost_estimate=pl.CostEstimate(
            flops=4 * rows * model * units * chunks, bytes_accessed=20 << 20, transcendentals=0
        ),
        name="experts",
    )(inputs, hidden_grad, first, *kept)


def swap_tensor(block, bit):
    size = lax.axis_size("tensor")
    return lax.ppermute(block, "tensor", [(i, i ^ bit) for i in range(size)])


def swap_dp(buffer):
    return lax.all_to_all(buffer, "dp", split_axis=0, concat_axis=0, tiled=True)


def swap_seqs(buffer):
    return lax.all_to_all(buffer, "tensor", split_axis=0, concat_axis=0, tiled=True)


def tie(*values):
    return lax.optimization_barrier(values)


def gather_dp(block):
    size, index = lax.axis_size("dp"), lax.axis_index("dp")
    found = block[None]
    bit = size // 2
    while bit:
        other = lax.ppermute(found, "dp", [(i, i ^ bit) for i in range(size)])
        upper = (index & bit) > 0
        pair = [jnp.where(upper, other, found), jnp.where(upper, found, other)]
        found = jnp.stack(pair, axis=1).reshape((-1,) + block.shape)
        bit //= 2
    return found


def sum_all(values):
    for axis in ("tensor", "dp"):
        size = lax.axis_size(axis)
        bit = 1
        while bit < size:
            values = values + lax.ppermute(values, axis, [(i, i ^ bit) for i in range(size)])
            bit *= 2
    return values


def by_xor(stack, index):
    pairs = jnp.concatenate([stack[1:2], stack[:1], stack[3:], stack[2:3]], axis=0)
    stack = jnp.where((index & 1) > 0, pairs, stack)
    return jnp.where((index & 2) > 0, jnp.concatenate([stack[2:], stack[:2]], axis=0), stack)


def local(
    block_input,
    cotangent,
    segment_ids,
    rel_bucket,
    expert_route,
    expert_slot,
    attn_gain,
    moe_gain,
    router_weight,
    rel_table,
    w_query,
    w_key,
    w_value,
    w_out,
    expert_in,
    expert_out,
):
    group_seqs, part_len, model_width = block_input.shape
    tensor_size = lax.axis_size("tensor")
    dp_size = lax.axis_size("dp")
    full_len = part_len * tensor_size
    seqs_here = group_seqs // tensor_size
    head_cols = w_query.shape[1]
    weight_rows = w_query.shape[0]
    heads_all = rel_table.shape[1]
    heads_here = heads_all // tensor_size
    head_size = head_cols // heads_here
    bucket_count = rel_table.shape[0]
    experts_all = router_weight.shape[1]
    tok_rows = group_seqs * part_len
    capacity = tok_rows * 15 // (8 * experts_all)
    half = capacity // 2
    padded = (half // 16 + 1) * 16
    half_size = experts_all * padded
    tiles = full_len // TILE
    me = lax.axis_index("tensor")

    packed = jnp.concatenate([w_query, w_key, w_value, w_out.T], axis=1)
    own_first = expert_in.reshape(model_width, -1)
    own_second = expert_out.reshape(-1, model_width)
    packed, tokens_in = tie(packed, block_input)
    w_own = gather_dp(packed).reshape(model_width, 4 * head_cols)
    w_core = swap_tensor(w_own, 1)
    w_far = swap_tensor(w_own, 2)

    flat_input = tokens_in.astype(F32)
    attn_gain_f = attn_gain.astype(F32)
    normed_local = attn_norm(flat_input, attn_gain_f).astype(BF)

    def by_seqs(rows):
        return swap_seqs(rows.reshape(tensor_size, seqs_here, part_len, model_width))

    n1_seqs = by_seqs(normed_local)
    seg_here = lax.dynamic_slice_in_dim(segment_ids, me * seqs_here, seqs_here, 0)
    bucket_onehot = (rel_bucket[:, None] == jnp.arange(bucket_count)[None, :]).astype(F32)
    bias_line = jnp.einsum(
        "kb,bh->hk", bucket_onehot, rel_table.astype(F32), precision=lax.Precision.HIGHEST
    )
    bias_line = jnp.pad(bias_line, ((0, 0), (1, 0))).reshape(heads_all, 2 * tiles, TILE)
    windows = jnp.concatenate([bias_line, jnp.roll(bias_line, -1, axis=1)], axis=2)
    windows = windows.reshape(tensor_size, heads_here, 2 * tiles, 2 * TILE)
    windows = by_xor(windows, me)

    route_rows = expert_route.reshape(tok_rows)
    slot_rows = expert_slot.reshape(tok_rows)
    upper = slot_rows >= half
    slot_place = jnp.where(
        slot_rows >= 0,
        route_rows * 2 * padded + slot_rows + upper * (padded - half),
        2 * half_size,
    )
    slot_ids = jnp.arange(2 * half_size).reshape(experts_all, 2, padded)

    def table_of(ids):
        return (slot_place[:, None] == ids.reshape(1, -1)).astype(BF)

    slot_tables = [table_of(slot_ids[:, h]) for h in range(2)]
    slot_table = table_of(slot_ids)
    route_onehot = (route_rows[:, None] == jnp.arange(experts_all)[None, :]).astype(F32)

    def place_rows(rows, h):
        placed = lax.dot_general(slot_tables[h], rows, TN, preferred_element_type=F32)
        return placed.reshape(experts_all, padded, model_width)

    def take_rows(buffers):
        return sum(
            matmul(slot_tables[h], buffers[h].reshape(half_size, -1)) for h in range(2)
        )

    def with_extra(placed, numbers, h):
        high = numbers.astype(BF)
        low = (numbers - high.astype(F32)).astype(BF)
        parts = lax.dot_general(jnp.stack([high, low]), slot_tables[h], (((1,), (0,)), ((), ())),
                                preferred_element_type=F32)
        parts = parts.reshape(2, experts_all, padded).transpose(1, 0, 2)
        parts = parts.reshape(experts_all, 1, 2 * padded)
        parts = jnp.pad(parts, ((0, 0), (0, 0), (0, model_width - 2 * padded)))
        at_extra = jnp.arange(padded)[None, :, None] == half
        return jnp.where(at_extra, parts, placed).astype(BF)

    def extra_of(buffer):
        row = buffer[:, half].astype(F32)
        return row[:, :padded] + row[:, padded : 2 * padded]

    cotangent_rows = cotangent.reshape(tok_rows, model_width)
    c_placed = lax.dot_general(slot_table, cotangent_rows, TN, preferred_element_type=F32)
    c_placed = c_placed.astype(BF).reshape(experts_all, 2 * padded, model_width)
    c_placed, n1_seqs, w_own = tie(c_placed, n1_seqs, w_own)
    c_arrived = swap_dp(c_placed)

    def stack_tensor(own, far):
        return jnp.stack([own, far, swap_tensor(own, 1), swap_tensor(far, 1)])

    partial, *kept_near = attend(
        me, n1_seqs, (w_own, w_core), seg_here, windows[:2], None, heads_here, head_size
    )
    partial, w_far, own_second = tie(partial, w_far, own_second)
    w_both = swap_tensor(w_far, 1)
    far_second = swap_tensor(own_second, 2)
    *branch, qkv_far, o_far, p_far = attend(
        me, n1_seqs, (w_far, w_both), seg_here, windows[2:], partial, heads_here, head_size
    )
    kept_far = (qkv_far, o_far, p_far)
    *branch, far_second = tie(*branch, far_second)
    branch = branch[:1] + [swap_tensor(branch[k], k) for k in range(1, 4)]
    *branch, c_arrived, own_first = tie(*branch, c_arrived, own_first)
    far_first = swap_tensor(own_first, 2)
    attn_branch = by_xor(jnp.stack(branch), me).reshape(tok_rows, model_width).astype(F32)
    hidden_rows = flat_input.reshape(tok_rows, model_width) + attn_branch

    moe_gain_f = moe_gain.astype(F32)
    router_f = router_weight.astype(F32)
    rms = rms_inverse(hidden_rows)
    scaled = hidden_rows * rms
    normed_moe = scaled * moe_gain_f
    logits = jnp.dot(
        normed_moe, router_f, precision=lax.Precision.HIGHEST, preferred_element_type=F32
    )
    router_probs = jax.nn.softmax(logits, axis=-1)
    gate_value = jnp.sum(router_probs * route_onehot, axis=-1)

    sent_rows = normed_moe.astype(BF)
    u_placed = [with_extra(place_rows(sent_rows, h), gate_value, h) for h in range(2)]
    u_first = swap_dp(u_placed[0])
    second = stack_tensor(own_second, far_second)
    c_all = c_arrived.reshape(experts_all, 2, padded, model_width)
    u_next, c_all = tie(u_placed[1], c_all)
    hidden_grad = hidden_grads(c_all, second)
    u_first, u_next, hidden_grad = tie(u_first, u_next, hidden_grad)
    u_second = swap_dp(u_next)
    hidden_grad, far_first = tie(hidden_grad, far_first)
    first = stack_tensor(own_first, far_first)
    back_first, *kept = run_experts(0, half, u_first, hidden_grad, first, ())
    back_second, hidden, pre_grad = run_experts(1, half, u_second, hidden_grad, first, kept)
    back_first, u_second = tie(back_first, u_second)
    back_first = swap_dp(back_first)
    out_rows = jnp.einsum(
        "krf,kfd->rd",
        hidden.reshape(tensor_size, 2 * half_size, -1),
        second,
        preferred_element_type=F32,
    )
    out_rows = out_rows.astype(BF).reshape(experts_all, 2 * padded, model_width)
    back_first, back_second, out_rows = tie(back_first, back_second, out_rows)
    back_second = swap_dp(back_second)

    gates = jnp.stack([extra_of(u_first), extra_of(u_second)], axis=1)[..., None]
    first_terms, first_near, second_terms, second_near = expert_grads(
        gates.reshape(2 * half_size, 1), u_first, u_second, c_all, hidden, pre_grad
    )

    def near_sum(own, near):
        return own.astype(F32) + swap_tensor(near, 1).astype(F32)

    def near_terms(stack, near):
        near = swap_tensor(near, 1)
        passed = (stack[1].astype(F32) + near[1].astype(F32)).astype(BF)
        return passed, stack[0], near[0]

    first_passed, *first_parts = near_terms(first_terms, first_near)
    second_passed, *second_parts = near_terms(second_terms, second_near)

    out_grad = cotangent_rows.astype(F32)
    back_second, first_terms = tie(back_second, first_terms)
    gate_back = [extra_of(back_first), extra_of(back_second)]
    gate_back = [
        jnp.stack([v.astype(BF), (v - v.astype(BF).astype(F32)).astype(BF)], axis=-1)
        for v in gate_back
    ]
    gate_grad = jnp.sum(take_rows(gate_back), axis=-1)
    logit_grad = (gate_grad * gate_value)[:, None] * (route_onehot - router_probs)
    normed_grad = gate_value[:, None] * take_rows([back_first, back_second]) + lax.dot_general(
        logit_grad, router_f, NT, precision=lax.Precision.HIGHEST, preferred_element_type=F32
    )
    gained = normed_grad * moe_gain_f
    residual_grad = (
        out_grad + rms * gained - scaled * rms * jnp.mean(gained * scaled, axis=-1, keepdims=True)
    )
    db_rows = residual_grad.astype(BF).reshape(tensor_size, seqs_here, part_len, model_width)
    db_rows, out_rows = tie(db_rows, out_rows)
    returned = swap_dp(out_rows)
    db_blocks = [lax.dynamic_index_in_dim(db_rows, me ^ k, 0, keepdims=False) for k in range(4)]
    db_blocks = db_blocks[:1] + [swap_tensor(db_blocks[k], k) for k in range(1, 4)]
    router_part = lax.dot_general(
        normed_moe, logit_grad, TN, precision=lax.Precision.HIGHEST, preferred_element_type=F32
    )
    moe_gain_part = jnp.sum(normed_grad * scaled, axis=0)
    *db_blocks, first_passed, router_part, moe_gain_part = tie(
        *db_blocks, first_passed, router_part, moe_gain_part
    )
    first_far = swap_tensor(first_passed, 2)

    partial, dw_far, dw_both, lines_far = attend_back(
        me, n1_seqs, db_blocks, kept_far, (w_far, w_both), None, heads_here, head_size
    )
    dw_both, first_far = tie(dw_both, first_far)
    first_grad = sum(v.astype(F32) for v in (*first_parts, first_far)).reshape(expert_in.shape)
    far_term = near_sum(dw_far, dw_both).astype(BF)
    partial, far_term, first_grad = tie(partial, far_term, first_grad)
    far_term = swap_tensor(far_term, 2)
    *normed_back, dw_own, dw_core, lines_near, gain_sums = attend_back(
        me, n1_seqs, db_blocks, kept_near, (w_own, w_core), partial, heads_here, head_size
    )
    dw_core, far_term, returned, second_passed = tie(dw_core, far_term, returned, second_passed)
    second_far = swap_tensor(second_passed, 2)
    owner_terms = (near_sum(dw_own, dw_core) + far_term.astype(F32)).astype(BF)
    owner_terms, gain_sums, lines_near, *normed_back = tie(
        owner_terms, gain_sums, lines_near, *normed_back
    )
    owner_terms = swap_dp(owner_terms.reshape(dp_size, weight_rows, 4 * head_cols))

    normed_back = normed_back[:1] + [swap_tensor(normed_back[k], k) for k in range(1, 4)]
    owner_terms, returned, *normed_back = tie(owner_terms, returned, *normed_back)
    normed_back = by_xor(jnp.stack(normed_back), me)
    normed_back = normed_back.reshape(group_seqs, part_len, model_width).astype(F32)
    gained_in = normed_back * attn_gain_f
    rms_in = rms_inverse(flat_input)
    scaled_in = flat_input * rms_in
    input_grad = (
        residual_grad.reshape(group_seqs, part_len, model_width)
        + rms_in * gained_in
        - scaled_in * rms_in * jnp.mean(gained_in * scaled_in, axis=-1, keepdims=True)
    )
    block_output = hidden_rows + gate_value[:, None] * matmul(
        slot_table, returned.reshape(2 * half_size, model_width)
    )
    block_output = block_output.astype(BF).reshape(group_seqs, part_len, model_width)
    block_output, input_grad, second_far = tie(block_output, input_grad, second_far)
    second_grad = sum(v.astype(F32) for v in (*second_parts, second_far))
    second_grad = second_grad.reshape(expert_out.shape)

    line_sums = by_xor(jnp.concatenate([lines_near, lines_far], axis=0), me)
    low, high = line_sums[..., :TILE], line_sums[..., TILE:]
    offset_sums = low + jnp.roll(high, 1, axis=2)
    offset_sums = offset_sums.reshape(heads_all, 2 * full_len)[:, 1:]
    table_part = jnp.einsum(
        "hk,kb->bh", offset_sums, bucket_onehot, precision=lax.Precision.HIGHEST
    )
    small = [gain_sums[0] / attn_gain_f, moe_gain_part, router_part, table_part]
    sums = jnp.concatenate([v.reshape(-1) for v in small])
    size = sums.size
    sums = jnp.pad(sums, (0, -size % (8 * TILE))).reshape(-1, TILE)
    sums = sum_all(sums).reshape(-1)
    owner_grad = jnp.sum(owner_terms.astype(F32), axis=0)
    totals, start = [], 0
    for v in small:
        totals.append(sums[start : start + v.size].reshape(v.shape))
        start += v.size
    return (
        block_output,
        input_grad,
        *totals,
        owner_grad[:, :head_cols],
        owner_grad[:, head_cols : 2 * head_cols],
        owner_grad[:, 2 * head_cols : 3 * head_cols],
        owner_grad[:, 3 * head_cols :].T,
        first_grad,
        second_grad,
    )


def solution(mesh):
    in_specs = (
        P("dp", "tensor", None),
        P("dp", "tensor", None),
        P("dp", None),
        P(),
        P("dp", "tensor"),
        P("dp", "tensor"),
        P(),
        P(),
        P(),
        P(),
        P("dp", "tensor"),
        P("dp", "tensor"),
        P("dp", "tensor"),
        P("tensor", "dp"),
        P("dp", None, "tensor"),
        P("dp", "tensor", None),
    )
    out_specs = (
        P("dp", "tensor", None),
        P("dp", "tensor", None),
        P(),
        P(),
        P(),
        P(),
        P("dp", "tensor"),
        P("dp", "tensor"),
        P("dp", "tensor"),
        P("tensor", "dp"),
        P("dp", None, "tensor"),
        P("dp", "tensor", None),
    )
    return jax.shard_map(local, mesh=mesh, in_specs=in_specs, out_specs=out_specs, check_vma=False)
```

```python
import functools

import jax
import jax.numpy as jnp
from jax import lax
from jax.experimental import pallas as pl
from jax.experimental.pallas import tpu as pltpu
from jax.sharding import PartitionSpec as P

EPSILON = 1e-06
MASKED_SCORE = -1e30
BF = jnp.bfloat16
F32 = jnp.float32
TILE = 128
NT = (((1,), (1,)), ((), ()))
TN = (((0,), (0,)), ((), ()))


def rms_inverse(values):
    return lax.rsqrt(jnp.mean(values * values, axis=-1, keepdims=True) + EPSILON)


def attn_norm(tokens_in, gain):
    return tokens_in * rms_inverse(tokens_in) * gain


def matmul(left, right, dims=None):
    if dims is None:
        dims = (((1,), (0,)), ((), ()))
    return lax.dot_general(left, right, dims, preferred_element_type=F32)


def head_only(rows, head, head_size):
    lane = lax.broadcasted_iota(jnp.int32, rows.shape, 1)
    inside = (lane >= head * head_size) & (lane < (head + 1) * head_size)
    return jnp.where(inside, rows, jnp.zeros_like(rows))


def attend_kernel(heads, head_size, has_base, last, *refs):
    me_ref, n1_ref, segc_ref, segr_ref, line_ref = refs[:5]
    w_refs, refs = refs[5:7], refs[7:]
    if has_base:
        base_ref, refs = refs[0], refs[1:]
    if last:
        out_refs, refs = refs[:4], refs[4:]
        refs, total_all = refs[:-1], refs[-1]
    else:
        out_ref, refs = refs[0], refs[1:]
    qkv_ref, o_ref, p_ref, bias_ref = refs
    seq = pl.program_id(0)
    width = heads * head_size
    model = n1_ref.shape[-1]
    length = segr_ref.shape[-1]
    tiles = length // TILE

    @pl.when(seq == 0)
    def _():
        for group in range(2):
            for head in range(heads):
                for d in range(2 * tiles - 1):
                    line = jnp.broadcast_to(line_ref[group, head, d : d + 1, :], (TILE, 2 * TILE))
                    tile = pltpu.roll(line, 0, 1, stride=1, stride_axis=0)[:, TILE:]
                    bias_ref[group, head, d] = tile

    rows = n1_ref[:, 0].reshape(length, model)
    seg_row = segr_ref[0]
    branch = None
    for group in range(2):
        qkv = matmul(rows, w_refs[group][:, : 3 * width]).astype(BF)
        qkv_ref[group, 0] = qkv
        queries, keys, values = qkv[:, :width], qkv[:, width : 2 * width], qkv[:, 2 * width :]
        attended = jnp.zeros((length, width), F32)
        for head in range(heads):
            scores = matmul(head_only(queries, head, head_size), keys, NT)
            for t in range(tiles):
                span = slice(t * TILE, (t + 1) * TILE)
                bias = jnp.concatenate(
                    [bias_ref[group, head, c - t + tiles - 1] for c in range(tiles)], axis=1
                )
                same_doc = segc_ref[0, span] == seg_row
                part = jnp.where(same_doc, scores[span] + bias, MASKED_SCORE)
                peak = jnp.max(part, axis=1, keepdims=True)
                expo = jnp.exp(part - peak)
                total = jnp.sum(expo, axis=1, keepdims=True)
                p_ref[group, 0, head, span] = (expo * (1.0 / total)).astype(BF)
            attended += matmul(p_ref[group, 0, head], head_only(values, head, head_size))
        attended = attended.astype(BF)
        o_ref[group, 0] = attended
        term = matmul(attended, w_refs[group][:, 3 * width :], NT)
        branch = term if branch is None else branch + term
    if has_base:
        branch = branch + base_ref[0]
    if last:
        total_all[...] = branch
        part_len = n1_ref.shape[2]
        for k in range(4):
            start = pl.multiple_of((me_ref[0] ^ k) * part_len, part_len)
            out_refs[k][0] = total_all[pl.ds(start, part_len)].astype(BF)
    else:
        out_ref[0] = branch


def attend_back_kernel(heads, head_size, has_base, last, *refs):
    me_ref, n1_ref, qkv_ref, o_ref, p_ref = refs[:5]
    w_refs, db_refs, refs = refs[5:7], refs[7:11], refs[11:]
    if has_base:
        base_ref, refs = refs[0], refs[1:]
    if last:
        out_refs, refs = refs[:4], refs[4:]
    else:
        out_ref, refs = refs[0], refs[1:]
    dw_refs, line_ref, refs = refs[:2], refs[2], refs[3:]
    if last:
        gain_ref, refs = refs[0], refs[1:]
    dw_acc, sums_ref, db_all, total_all = refs
    seq = pl.program_id(0)
    part_len = n1_ref.shape[2]

    def place_of(k):
        return pl.ds(pl.multiple_of((me_ref[0] ^ k) * part_len, part_len), part_len)

    for k in range(4):
        db_all[place_of(k)] = db_refs[k][0]
    width = heads * head_size
    model = n1_ref.shape[-1]
    length = qkv_ref.shape[2]
    tiles = length // TILE
    rows = n1_ref[:, 0].reshape(length, model)
    branch_grad = db_all[...]

    @pl.when(seq == 0)
    def _():
        sums_ref[...] = jnp.zeros_like(sums_ref)
        dw_acc[...] = jnp.zeros_like(dw_acc)
        if last:
            gain_ref[...] = jnp.zeros_like(gain_ref)

    total = None
    for group in range(2):
        w_ref = w_refs[group]
        attended_grad = matmul(branch_grad, w_ref[:, 3 * width :]).astype(BF)
        qkv = qkv_ref[group, 0]
        queries, keys, values = qkv[:, :width], qkv[:, width : 2 * width], qkv[:, 2 * width :]
        attended = o_ref[group, 0]
        queries_t = queries.T
        grad_t = attended_grad.T
        inner_all = attended_grad.astype(F32) * attended.astype(F32)
        query_grad = jnp.zeros((length, width), F32)
        key_grads, value_grads = [], []
        for head in range(heads):
            cut = slice(head * head_size, (head + 1) * head_size)
            inner = jnp.sum(head_only(inner_all, head, head_size), axis=1, keepdims=True)
            prob_grad = matmul(head_only(attended_grad, head, head_size), values, NT)
            probs = p_ref[group, 0, head]
            parts = []
            for t in range(tiles):
                span = slice(t * TILE, (t + 1) * TILE)
                part = probs[span].astype(F32) * (prob_grad[span] - inner[span])
                for c in range(tiles):
                    tile = part[:, c * TILE : (c + 1) * TILE]
                    sums_ref[group, head, c - t + tiles - 1] += tile
                parts.append(part.astype(BF))
            score_grad = jnp.concatenate(parts, axis=0)
            query_grad += matmul(score_grad, head_only(keys, head, head_size))
            key_grads.append(matmul(queries_t[cut], score_grad))
            value_grads.append(matmul(grad_t[cut], probs))
        key_grad = jnp.concatenate(key_grads, axis=0).T
        value_grad = jnp.concatenate(value_grads, axis=0).T
        joined = jnp.concatenate(
            [query_grad.astype(BF), key_grad.astype(BF), value_grad.astype(BF)], axis=1
        )
        term = matmul(joined, w_ref[:, : 3 * width], NT)
        total = term if total is None else total + term
        dw_acc[group, :, : 3 * width] += matmul(rows, joined, TN)
        dw_acc[group, :, 3 * width :] += matmul(branch_grad, attended, TN)
    if has_base:
        total = total + base_ref[0]
    if last:
        total_all[...] = total
        for k in range(4):
            out_refs[k][0] = total_all[place_of(k)].astype(BF)
        gain_ref[...] += jnp.sum(total * rows.astype(F32), axis=0, keepdims=True)
    else:
        out_ref[0] = total

    @pl.when(seq == pl.num_programs(0) - 1)
    def _():
        row = lax.broadcasted_iota(jnp.int32, (TILE, TILE), 0)
        lane = lax.broadcasted_iota(jnp.int32, (TILE, TILE), 1)
        flip = (row + lane == TILE - 1).astype(F32)
        for group in range(2):
            dw_refs[group][...] = dw_acc[group].astype(BF)
            for head in range(heads):
                for d in range(2 * tiles - 1):
                    turned = lax.dot_general(
                        flip, sums_ref[group, head, d], (((1,), (0,)), ((), ())),
                        precision=lax.Precision.HIGHEST, preferred_element_type=F32,
                    )
                    wide = jnp.concatenate([turned, jnp.zeros_like(turned)], axis=1)
                    skewed = pltpu.roll(wide, 1, 1, stride=1, stride_axis=0)
                    line_ref[group, head, d : d + 1, :] = jnp.sum(skewed, axis=0, keepdims=True)
                line_ref[group, head, 2 * tiles - 1 :, :] = jnp.zeros((1, 2 * TILE), F32)


def expert_kernel(slots, u_ref, hg_ref, wi_ref, *refs):
    du_ref, r_ref, da_ref, acc_ref, dg_acc = refs[-5:]
    chunk = pl.program_id(1)
    first = wi_ref[0]
    sources, padded, model = u_ref.shape
    pre_act = matmul(u_ref[...].reshape(sources * padded, model), first)
    hidden_grad = hg_ref[0, :, 0].reshape(sources * padded, -1).astype(F32)
    root = 0.7978845608028654
    square = pre_act * pre_act
    bend = jnp.tanh(root * pre_act * (1.0 + 0.044715 * square))
    half = 0.5 * (1.0 + bend)
    hidden = (pre_act * half).astype(BF)
    slope = half + 0.5 * root * pre_act * (1.0 - bend * bend) * (1.0 + 3 * 0.044715 * square)
    pre_grad = (hidden_grad * slope).astype(BF)
    r_ref[0, :, 0] = hidden.reshape(sources, padded, -1)
    da_ref[0, :, 0] = pre_grad.reshape(sources, padded, -1)
    gate_part = jnp.sum(hidden.astype(F32) * hidden_grad, axis=1, keepdims=True)
    input_part = matmul(pre_grad, first, NT)

    @pl.when(chunk == 0)
    def _():
        acc_ref[...] = input_part
        dg_acc[...] = gate_part

    @pl.when(chunk > 0)
    def _():
        acc_ref[...] += input_part
        dg_acc[...] += gate_part

    @pl.when(chunk == pl.num_programs(1) - 1)
    def _():
        gates = jnp.broadcast_to(dg_acc[...], (sources * padded, TILE)).T[0:1]
        place = lax.broadcasted_iota(jnp.int32, (padded, model), 0)
        for source in range(sources):
            span = slice(source * padded, (source + 1) * padded)
            gate = gates[:, span]
            high = gate.astype(BF).astype(F32)
            extra = jnp.concatenate(
                [high, gate - high, jnp.zeros((1, model - 2 * padded), F32)], axis=1
            )
            du_ref[source] = jnp.where(place == slots, extra, acc_ref[span]).astype(BF)


def attend(me, n1_seqs, weights, seg_here, lines, base, heads, head_size):
    groups, seqs, part, model = n1_seqs.shape
    length = seg_here.shape[1]
    width = heads * head_size
    tiles = length // TILE
    last = base is not None
    flops = 2 * 2 * seqs * length * (4 * width * model + 2 * heads * length * head_size)
    whole = pl.BlockSpec((model, 4 * width), lambda s: (0, 0))
    rows_spec = pl.BlockSpec((1, length, model), lambda s: (s, 0, 0))
    seqs_spec = pl.BlockSpec((groups, 1, part, model), lambda s: (0, s, 0, 0))
    block_spec = pl.BlockSpec((1, part, model), lambda s: (s, 0, 0))
    return pl.pallas_call(
        functools.partial(attend_kernel, heads, head_size, last, last),
        grid=(seqs,),
        in_specs=[
            pl.BlockSpec(memory_space=pltpu.SMEM),
            seqs_spec,
            pl.BlockSpec((1, length, 1), lambda s: (s, 0, 0)),
            pl.BlockSpec((1, 1, length), lambda s: (s, 0, 0)),
            pl.BlockSpec((2, heads, 2 * tiles, 2 * TILE), lambda s: (0, 0, 0, 0)),
            whole,
            whole,
        ]
        + [rows_spec] * last,
        out_specs=[block_spec] * 4 * last
        + [rows_spec] * (not last)
        + [
            pl.BlockSpec((2, 1, length, 3 * width), lambda s: (0, s, 0, 0)),
            pl.BlockSpec((2, 1, length, width), lambda s: (0, s, 0, 0)),
            pl.BlockSpec((2, 1, heads, length, length), lambda s: (0, s, 0, 0, 0)),
        ],
        out_shape=[jax.ShapeDtypeStruct((seqs, part, model), BF)] * 4 * last
        + [jax.ShapeDtypeStruct((seqs, length, model), F32)] * (not last)
        + [
            jax.ShapeDtypeStruct((2, seqs, length, 3 * width), BF),
            jax.ShapeDtypeStruct((2, seqs, length, width), BF),
            jax.ShapeDtypeStruct((2, seqs, heads, length, length), BF),
        ],
        scratch_shapes=[pltpu.VMEM((2, heads, 2 * tiles - 1, TILE, TILE), F32)]
        + [pltpu.VMEM((length, model), F32)] * last,
        compiler_params=pltpu.CompilerParams(vmem_limit_bytes=48 << 20),
        cost_estimate=pl.CostEstimate(
            flops=3 * flops, bytes_accessed=12 << 20, transcendentals=2 * seqs * heads * length**2
        ),
        name="attend",
    )(me.reshape(1), n1_seqs, seg_here[:, :, None], seg_here[:, None, :], lines, *weights, *([base] * last))


def attend_back(me, n1_seqs, db_blocks, kept, weights, base, heads, head_size):
    qkv, attended, probs = kept
    groups, seqs, part, model = n1_seqs.shape
    length = qkv.shape[2]
    width = heads * head_size
    tiles = length // TILE
    last = base is not None
    flops = 2 * 2 * seqs * length * (8 * width * model + 4 * heads * length * head_size)
    whole = pl.BlockSpec((model, 4 * width), lambda s: (0, 0))
    rows_spec = pl.BlockSpec((1, length, model), lambda s: (s, 0, 0))
    seqs_spec = pl.BlockSpec((groups, 1, part, model), lambda s: (0, s, 0, 0))
    block_spec = pl.BlockSpec((1, part, model), lambda s: (s, 0, 0))
    dw_shape = jax.ShapeDtypeStruct((model, 4 * width), BF)
    return pl.pallas_call(
        functools.partial(attend_back_kernel, heads, head_size, last, last),
        grid=(seqs,),
        in_specs=[
            pl.BlockSpec(memory_space=pltpu.SMEM),
            seqs_spec,
            pl.BlockSpec((2, 1, length, 3 * width), lambda s: (0, s, 0, 0)),
            pl.BlockSpec((2, 1, length, width), lambda s: (0, s, 0, 0)),
            pl.BlockSpec((2, 1, heads, length, length), lambda s: (0, s, 0, 0, 0)),
            whole,
            whole,
        ]
        + [block_spec] * 4
        + [rows_spec] * last,
        out_specs=[block_spec] * 4 * last
        + [rows_spec] * (not last)
        + [
            whole,
            whole,
            pl.BlockSpec((2, heads, 2 * tiles, 2 * TILE), lambda s: (0, 0, 0, 0)),
        ]
        + [pl.BlockSpec((1, model), lambda s: (0, 0))] * last,
        out_shape=[jax.ShapeDtypeStruct((seqs, part, model), BF)] * 4 * last
        + [jax.ShapeDtypeStruct((seqs, length, model), F32)] * (not last)
        + [
            dw_shape,
            dw_shape,
            jax.ShapeDtypeStruct((2, heads, 2 * tiles, 2 * TILE), F32),
        ]
        + [jax.ShapeDtypeStruct((1, model), F32)] * last,
        scratch_shapes=[
            pltpu.VMEM((2, model, 4 * width), F32),
            pltpu.VMEM((2, heads, 2 * tiles - 1, TILE, TILE), F32),
            pltpu.VMEM((length, model), BF),
            pltpu.VMEM((length, model), F32),
        ],
        compiler_params=pltpu.CompilerParams(vmem_limit_bytes=56 << 20),
        cost_estimate=pl.CostEstimate(
            flops=2 * flops, bytes_accessed=16 << 20, transcendentals=0
        ),
        name="attend_back",
    )(me.reshape(1), n1_seqs, qkv, attended, probs, *weights, *db_blocks, *([base] * last))


def hidden_grads_kernel(c_ref, wo_ref, hg_ref):
    experts, halves, padded, model = c_ref.shape
    units = wo_ref.shape[1]
    grads = matmul(c_ref[...].reshape(experts * halves * padded, model), wo_ref[0], NT)
    hg_ref[0] = grads.astype(BF).reshape(experts, halves, padded, units)


def hidden_grads(grads, second):
    experts, halves, padded, model = grads.shape
    chunks, units, _ = second.shape
    sources = experts // 2
    return pl.pallas_call(
        hidden_grads_kernel,
        grid=(chunks, experts // sources),
        in_specs=[
            pl.BlockSpec((sources, halves, padded, model), lambda k, b: (b, 0, 0, 0)),
            pl.BlockSpec((1, units, model), lambda k, b: (k, 0, 0)),
        ],
        out_specs=pl.BlockSpec((1, sources, halves, padded, units), lambda k, b: (k, b, 0, 0, 0)),
        out_shape=jax.ShapeDtypeStruct((chunks, experts, halves, padded, units), BF),
        compiler_params=pltpu.CompilerParams(vmem_limit_bytes=48 << 20),
        cost_estimate=pl.CostEstimate(flops=1, bytes_accessed=1, transcendentals=0),
        name="hidden_grads",
    )(grads, second)


def expert_grads_kernel(gate_ref, ua_ref, ub_ref, c_ref, r_ref, da_ref,
                        di_ref, di_near, do_ref, do_near, u_t, c_t, di_acc, do_acc):
    chunk, step = pl.program_id(0), pl.program_id(1)
    experts, halves, padded, model = c_ref.shape
    sources = experts // 2
    rows = sources * halves * padded
    units = r_ref.shape[-1]

    @pl.when(chunk == 0)
    def _():
        start = step * sources
        gate = gate_ref[pl.ds(pl.multiple_of(step * rows, rows), rows)]
        ua, ub = ua_ref[pl.ds(start, sources)], ub_ref[pl.ds(start, sources)]
        inputs = jnp.concatenate([ua[:, None], ub[:, None]], axis=1).reshape(rows, model)
        u_t[step] = (inputs.astype(F32) * gate).astype(BF).T
        grads = c_ref[pl.ds(start, sources)].reshape(rows, model)
        c_t[step] = (grads.astype(F32) * gate).astype(BF).T

    hidden = r_ref[0].reshape(rows, units)
    second_part = matmul(c_t[step], hidden)
    first_part = matmul(u_t[step], da_ref[0].reshape(rows, units))

    @pl.when(step == 0)
    def _():
        di_acc[...] = first_part
        do_acc[...] = second_part

    @pl.when((step == 1) & (chunk < 2))
    def _():
        di_ref[0] = (di_acc[...] + first_part).astype(BF)
        do_ref[0] = (do_acc[...] + second_part).T.astype(BF)

    @pl.when((step == 1) & (chunk >= 2))
    def _():
        di_near[0] = (di_acc[...] + first_part).astype(BF)
        do_near[0] = (do_acc[...] + second_part).T.astype(BF)


def expert_grads(gates, u_first, u_second, grads, hidden, pre_grad):
    experts, halves, padded, model = grads.shape
    chunks, units = hidden.shape[0], hidden.shape[-1]
    sources = experts // 2
    rows = sources * halves * padded

    def whole(array):
        zeros = (0,) * array.ndim
        return pl.BlockSpec(array.shape, lambda k, b: zeros, pipeline_mode=pl.Buffered(1))

    kept_spec = pl.BlockSpec((1, sources, halves, padded, units), lambda k, b: (k, b, 0, 0, 0))
    own = pl.BlockSpec((1, model, units), lambda k, b: (jnp.minimum(k, 1), 0, 0))
    near = pl.BlockSpec((1, model, units), lambda k, b: (jnp.maximum(k - 2, 0), 0, 0))
    return pl.pallas_call(
        expert_grads_kernel,
        grid=(chunks, 2),
        in_specs=[
            whole(gates),
            whole(u_first),
            whole(u_second),
            whole(grads),
            kept_spec,
            kept_spec,
        ],
        out_specs=[
            own,
            near,
            own,
            near,
        ],
        out_shape=[jax.ShapeDtypeStruct((2, model, units), BF)] * 4,
        scratch_shapes=[
            pltpu.VMEM((2, model, rows), BF),
            pltpu.VMEM((2, model, rows), BF),
            pltpu.VMEM((model, units), F32),
            pltpu.VMEM((model, units), F32),
        ],
        compiler_params=pltpu.CompilerParams(vmem_limit_bytes=60 << 20),
        cost_estimate=pl.CostEstimate(
            flops=8 * rows * model * units * chunks, bytes_accessed=40 << 20, transcendentals=0
        ),
        name="expert_grads",
    )(gates, u_first, u_second, grads, hidden, pre_grad)


def run_experts(half, slots, inputs, hidden_grad, first, kept):
    experts, padded, model = inputs.shape
    chunks, _, units = first.shape
    rows = experts * padded
    blocks = 2
    block = rows // blocks
    sources = experts // blocks
    kept_spec = pl.BlockSpec(
        (1, sources, 1, padded, units), lambda b, k: (k, b, half, 0, 0)
    )
    kept_shape = jax.ShapeDtypeStruct((chunks, experts, 2, padded, units), BF)
    return pl.pallas_call(
        functools.partial(expert_kernel, slots),
        grid=(blocks, chunks),
        in_specs=[
            pl.BlockSpec((sources, padded, model), lambda b, k: (b, 0, 0)),
            kept_spec,
            pl.BlockSpec((1, model, units), lambda b, k: (k, 0, 0)),
        ]
        + [pl.BlockSpec(memory_space=pl.ANY)] * len(kept),
        out_specs=[
            pl.BlockSpec((sources, padded, model), lambda b, k: (b, 0, 0)),
            kept_spec,
            kept_spec,
        ],
        out_shape=[jax.ShapeDtypeStruct((experts, padded, model), BF), kept_shape, kept_shape],
        scratch_shapes=[pltpu.VMEM((block, model), F32), pltpu.VMEM((block, 1), F32)],
        input_output_aliases={3 + i: 1 + i for i in range(len(kept))},
        compiler_params=pltpu.CompilerParams(vmem_limit_bytes=48 << 20),
        cost_estimate=pl.CostEstimate(
            flops=4 * rows * model * units * chunks, bytes_accessed=20 << 20, transcendentals=0
        ),
        name="experts",
    )(inputs, hidden_grad, first, *kept)


def swap_tensor(block, bit):
    size = lax.axis_size("tensor")
    return lax.ppermute(block, "tensor", [(i, i ^ bit) for i in range(size)])


def swap_dp(buffer):
    return lax.all_to_all(buffer, "dp", split_axis=0, concat_axis=0, tiled=True)


def swap_seqs(buffer):
    return lax.all_to_all(buffer, "tensor", split_axis=0, concat_axis=0, tiled=True)


def tie(*values):
    return lax.optimization_barrier(values)


def gather_dp(block):
    size, index = lax.axis_size("dp"), lax.axis_index("dp")
    found = block[None]
    bit = size // 2
    while bit:
        other = lax.ppermute(found, "dp", [(i, i ^ bit) for i in range(size)])
        upper = (index & bit) > 0
        pair = [jnp.where(upper, other, found), jnp.where(upper, found, other)]
        found = jnp.stack(pair, axis=1).reshape((-1,) + block.shape)
        bit //= 2
    return found


def sum_all(values):
    for axis in ("tensor", "dp"):
        size = lax.axis_size(axis)
        bit = 1
        while bit < size:
            values = values + lax.ppermute(values, axis, [(i, i ^ bit) for i in range(size)])
            bit *= 2
    return values


def by_xor(stack, index):
    pairs = jnp.concatenate([stack[1:2], stack[:1], stack[3:], stack[2:3]], axis=0)
    stack = jnp.where((index & 1) > 0, pairs, stack)
    return jnp.where((index & 2) > 0, jnp.concatenate([stack[2:], stack[:2]], axis=0), stack)


def local(
    block_input,
    cotangent,
    segment_ids,
    rel_bucket,
    expert_route,
    expert_slot,
    attn_gain,
    moe_gain,
    router_weight,
    rel_table,
    w_query,
    w_key,
    w_value,
    w_out,
    expert_in,
    expert_out,
):
    group_seqs, part_len, model_width = block_input.shape
    tensor_size = lax.axis_size("tensor")
    dp_size = lax.axis_size("dp")
    full_len = part_len * tensor_size
    seqs_here = group_seqs // tensor_size
    head_cols = w_query.shape[1]
    weight_rows = w_query.shape[0]
    heads_all = rel_table.shape[1]
    heads_here = heads_all // tensor_size
    head_size = head_cols // heads_here
    bucket_count = rel_table.shape[0]
    experts_all = router_weight.shape[1]
    tok_rows = group_seqs * part_len
    capacity = tok_rows * 15 // (8 * experts_all)
    half = capacity // 2
    padded = (half // 16 + 1) * 16
    half_size = experts_all * padded
    tiles = full_len // TILE
    me = lax.axis_index("tensor")

    packed = jnp.concatenate([w_query, w_key, w_value, w_out.T], axis=1)
    own_first = expert_in.reshape(model_width, -1)
    own_second = expert_out.reshape(-1, model_width)
    packed, tokens_in = tie(packed, block_input)
    w_own = gather_dp(packed).reshape(model_width, 4 * head_cols)
    w_core = swap_tensor(w_own, 1)
    w_far = swap_tensor(w_own, 2)

    flat_input = tokens_in.astype(F32)
    attn_gain_f = attn_gain.astype(F32)
    normed_local = attn_norm(flat_input, attn_gain_f).astype(BF)

    def by_seqs(rows):
        return swap_seqs(rows.reshape(tensor_size, seqs_here, part_len, model_width))

    n1_seqs = by_seqs(normed_local)
    seg_here = lax.dynamic_slice_in_dim(segment_ids, me * seqs_here, seqs_here, 0)
    bucket_onehot = (rel_bucket[:, None] == jnp.arange(bucket_count)[None, :]).astype(F32)
    bias_line = jnp.einsum(
        "kb,bh->hk", bucket_onehot, rel_table.astype(F32), precision=lax.Precision.HIGHEST
    )
    bias_line = jnp.pad(bias_line, ((0, 0), (1, 0))).reshape(heads_all, 2 * tiles, TILE)
    windows = jnp.concatenate([bias_line, jnp.roll(bias_line, -1, axis=1)], axis=2)
    windows = windows.reshape(tensor_size, heads_here, 2 * tiles, 2 * TILE)
    windows = by_xor(windows, me)

    route_rows = expert_route.reshape(tok_rows)
    slot_rows = expert_slot.reshape(tok_rows)
    upper = slot_rows >= half
    slot_place = jnp.where(
        slot_rows >= 0,
        route_rows * 2 * padded + slot_rows + upper * (padded - half),
        2 * half_size,
    )
    slot_ids = jnp.arange(2 * half_size).reshape(experts_all, 2, padded)

    def table_of(ids):
        return (slot_place[:, None] == ids.reshape(1, -1)).astype(BF)

    slot_tables = [table_of(slot_ids[:, h]) for h in range(2)]
    slot_table = table_of(slot_ids)
    route_onehot = (route_rows[:, None] == jnp.arange(experts_all)[None, :]).astype(F32)

    def place_rows(rows, h):
        placed = lax.dot_general(slot_tables[h], rows, TN, preferred_element_type=F32)
        return placed.reshape(experts_all, padded, model_width)

    def take_rows(buffers):
        return sum(
            matmul(slot_tables[h], buffers[h].reshape(half_size, -1)) for h in range(2)
        )

    def with_extra(placed, numbers, h):
        high = numbers.astype(BF)
        low = (numbers - high.astype(F32)).astype(BF)
        parts = lax.dot_general(jnp.stack([high, low]), slot_tables[h], (((1,), (0,)), ((), ())),
                                preferred_element_type=F32)
        parts = parts.reshape(2, experts_all, padded).transpose(1, 0, 2)
        parts = parts.reshape(experts_all, 1, 2 * padded)
        parts = jnp.pad(parts, ((0, 0), (0, 0), (0, model_width - 2 * padded)))
        at_extra = jnp.arange(padded)[None, :, None] == half
        return jnp.where(at_extra, parts, placed).astype(BF)

    def extra_of(buffer):
        row = buffer[:, half].astype(F32)
        return row[:, :padded] + row[:, padded : 2 * padded]

    cotangent_rows = cotangent.reshape(tok_rows, model_width)
    c_placed = lax.dot_general(slot_table, cotangent_rows, TN, preferred_element_type=F32)
    c_placed = c_placed.astype(BF).reshape(experts_all, 2 * padded, model_width)
    c_placed, n1_seqs, w_own = tie(c_placed, n1_seqs, w_own)
    c_arrived = swap_dp(c_placed)

    def stack_tensor(own, far):
        return jnp.stack([own, far, swap_tensor(own, 1), swap_tensor(far, 1)])

    partial, *kept_near = attend(
        me, n1_seqs, (w_own, w_core), seg_here, windows[:2], None, heads_here, head_size
    )
    partial, w_far, own_second = tie(partial, w_far, own_second)
    w_both = swap_tensor(w_far, 1)
    far_second = swap_tensor(own_second, 2)
    *branch, qkv_far, o_far, p_far = attend(
        me, n1_seqs, (w_far, w_both), seg_here, windows[2:], partial, heads_here, head_size
    )
    kept_far = (qkv_far, o_far, p_far)
    *branch, far_second = tie(*branch, far_second)
    branch = branch[:1] + [swap_tensor(branch[k], k) for k in range(1, 4)]
    *branch, c_arrived, own_first = tie(*branch, c_arrived, own_first)
    far_first = swap_tensor(own_first, 2)
    attn_branch = by_xor(jnp.stack(branch), me).reshape(tok_rows, model_width).astype(F32)
    hidden_rows = flat_input.reshape(tok_rows, model_width) + attn_branch

    moe_gain_f = moe_gain.astype(F32)
    router_f = router_weight.astype(F32)
    rms = rms_inverse(hidden_rows)
    scaled = hidden_rows * rms
    normed_moe = scaled * moe_gain_f
    logits = jnp.dot(
        normed_moe, router_f, precision=lax.Precision.HIGHEST, preferred_element_type=F32
    )
    router_probs = jax.nn.softmax(logits, axis=-1)
    gate_value = jnp.sum(router_probs * route_onehot, axis=-1)

    sent_rows = normed_moe.astype(BF)
    u_placed = [with_extra(place_rows(sent_rows, h), gate_value, h) for h in range(2)]
    u_first = swap_dp(u_placed[0])
    second = stack_tensor(own_second, far_second)
    c_all = c_arrived.reshape(experts_all, 2, padded, model_width)
    u_next, c_all = tie(u_placed[1], c_all)
    hidden_grad = hidden_grads(c_all, second)
    u_first, u_next, hidden_grad = tie(u_first, u_next, hidden_grad)
    u_second = swap_dp(u_next)
    hidden_grad, far_first = tie(hidden_grad, far_first)
    first = stack_tensor(own_first, far_first)
    back_first, *kept = run_experts(0, half, u_first, hidden_grad, first, ())
    back_second, hidden, pre_grad = run_experts(1, half, u_second, hidden_grad, first, kept)
    back_first, u_second = tie(back_first, u_second)
    back_first = swap_dp(back_first)
    out_rows = jnp.einsum(
        "krf,kfd->rd",
        hidden.reshape(tensor_size, 2 * half_size, -1),
        second,
        preferred_element_type=F32,
    )
    out_rows = out_rows.astype(BF).reshape(experts_all, 2 * padded, model_width)
    back_first, back_second, out_rows = tie(back_first, back_second, out_rows)
    back_second = swap_dp(back_second)

    gates = jnp.stack([extra_of(u_first), extra_of(u_second)], axis=1)[..., None]
    first_terms, first_near, second_terms, second_near = expert_grads(
        gates.reshape(2 * half_size, 1), u_first, u_second, c_all, hidden, pre_grad
    )

    def near_sum(own, near):
        return own.astype(F32) + swap_tensor(near, 1).astype(F32)

    def near_terms(stack, near):
        near = swap_tensor(near, 1)
        passed = (stack[1].astype(F32) + near[1].astype(F32)).astype(BF)
        return passed, stack[0], near[0]

    first_passed, *first_parts = near_terms(first_terms, first_near)
    second_passed, *second_parts = near_terms(second_terms, second_near)

    out_grad = cotangent_rows.astype(F32)
    back_second, first_terms = tie(back_second, first_terms)
    gate_back = [extra_of(back_first), extra_of(back_second)]
    gate_back = [
        jnp.stack([v.astype(BF), (v - v.astype(BF).astype(F32)).astype(BF)], axis=-1)
        for v in gate_back
    ]
    gate_grad = jnp.sum(take_rows(gate_back), axis=-1)
    logit_grad = (gate_grad * gate_value)[:, None] * (route_onehot - router_probs)
    normed_grad = gate_value[:, None] * take_rows([back_first, back_second]) + lax.dot_general(
        logit_grad, router_f, NT, precision=lax.Precision.HIGHEST, preferred_element_type=F32
    )
    gained = normed_grad * moe_gain_f
    residual_grad = (
        out_grad + rms * gained - scaled * rms * jnp.mean(gained * scaled, axis=-1, keepdims=True)
    )
    db_rows = residual_grad.astype(BF).reshape(tensor_size, seqs_here, part_len, model_width)
    db_rows, out_rows = tie(db_rows, out_rows)
    returned = swap_dp(out_rows)
    db_blocks = [lax.dynamic_index_in_dim(db_rows, me ^ k, 0, keepdims=False) for k in range(4)]
    db_blocks = db_blocks[:1] + [swap_tensor(db_blocks[k], k) for k in range(1, 4)]
    router_part = lax.dot_general(
        normed_moe, logit_grad, TN, precision=lax.Precision.HIGHEST, preferred_element_type=F32
    )
    moe_gain_part = jnp.sum(normed_grad * scaled, axis=0)
    *db_blocks, first_passed, router_part, moe_gain_part = tie(
        *db_blocks, first_passed, router_part, moe_gain_part
    )
    first_far = swap_tensor(first_passed, 2)

    partial, dw_far, dw_both, lines_far = attend_back(
        me, n1_seqs, db_blocks, kept_far, (w_far, w_both), None, heads_here, head_size
    )
    dw_both, first_far = tie(dw_both, first_far)
    first_grad = sum(v.astype(F32) for v in (*first_parts, first_far)).reshape(expert_in.shape)
    far_term = near_sum(dw_far, dw_both).astype(BF)
    partial, far_term, first_grad = tie(partial, far_term, first_grad)
    far_term = swap_tensor(far_term, 2)
    *normed_back, dw_own, dw_core, lines_near, gain_sums = attend_back(
        me, n1_seqs, db_blocks, kept_near, (w_own, w_core), partial, heads_here, head_size
    )
    dw_core, far_term, returned, second_passed = tie(dw_core, far_term, returned, second_passed)
    second_far = swap_tensor(second_passed, 2)
    owner_terms = (near_sum(dw_own, dw_core) + far_term.astype(F32)).astype(BF)
    owner_terms, gain_sums, lines_near, *normed_back = tie(
        owner_terms, gain_sums, lines_near, *normed_back
    )
    owner_terms = swap_dp(owner_terms.reshape(dp_size, weight_rows, 4 * head_cols))

    normed_back = normed_back[:1] + [swap_tensor(normed_back[k], k) for k in range(1, 4)]
    owner_terms, second_far, *normed_back = tie(owner_terms, second_far, *normed_back)
    normed_back = by_xor(jnp.stack(normed_back), me)
    normed_back = normed_back.reshape(group_seqs, part_len, model_width).astype(F32)
    gained_in = normed_back * attn_gain_f
    rms_in = rms_inverse(flat_input)
    scaled_in = flat_input * rms_in
    input_grad = (
        residual_grad.reshape(group_seqs, part_len, model_width)
        + rms_in * gained_in
        - scaled_in * rms_in * jnp.mean(gained_in * scaled_in, axis=-1, keepdims=True)
    )
    block_output = hidden_rows + gate_value[:, None] * matmul(
        slot_table, returned.reshape(2 * half_size, model_width)
    )
    block_output = block_output.astype(BF).reshape(group_seqs, part_len, model_width)
    second_grad = sum(v.astype(F32) for v in (*second_parts, second_far))
    second_grad = second_grad.reshape(expert_out.shape)

    line_sums = by_xor(jnp.concatenate([lines_near, lines_far], axis=0), me)
    low, high = line_sums[..., :TILE], line_sums[..., TILE:]
    offset_sums = low + jnp.roll(high, 1, axis=2)
    offset_sums = offset_sums.reshape(heads_all, 2 * full_len)[:, 1:]
    table_part = jnp.einsum(
        "hk,kb->bh", offset_sums, bucket_onehot, precision=lax.Precision.HIGHEST
    )
    small = [gain_sums[0] / attn_gain_f, moe_gain_part, router_part, table_part]
    sums = jnp.concatenate([v.reshape(-1) for v in small])
    size = sums.size
    sums = jnp.pad(sums, (0, -size % (8 * TILE))).reshape(-1, TILE)
    sums = sum_all(sums).reshape(-1)
    owner_grad = jnp.sum(owner_terms.astype(F32), axis=0)
    totals, start = [], 0
    for v in small:
        totals.append(sums[start : start + v.size].reshape(v.shape))
        start += v.size
    return (
        block_output,
        input_grad,
        *totals,
        owner_grad[:, :head_cols],
        owner_grad[:, head_cols : 2 * head_cols],
        owner_grad[:, 2 * head_cols : 3 * head_cols],
        owner_grad[:, 3 * head_cols :].T,
        first_grad,
        second_grad,
    )


def solution(mesh):
    in_specs = (
        P("dp", "tensor", None),
        P("dp", "tensor", None),
        P("dp", None),
        P(),
        P("dp", "tensor"),
        P("dp", "tensor"),
        P(),
        P(),
        P(),
        P(),
        P("dp", "tensor"),
        P("dp", "tensor"),
        P("dp", "tensor"),
        P("tensor", "dp"),
        P("dp", None, "tensor"),
        P("dp", "tensor", None),
    )
    out_specs = (
        P("dp", "tensor", None),
        P("dp", "tensor", None),
        P(),
        P(),
        P(),
        P(),
        P("dp", "tensor"),
        P("dp", "tensor"),
        P("dp", "tensor"),
        P("tensor", "dp"),
        P("dp", None, "tensor"),
        P("dp", "tensor", None),
    )
    return jax.shard_map(local, mesh=mesh, in_specs=in_specs, out_specs=out_specs, check_vma=False)
```
